128 devices in a mesh: grp: 8 (over y, core), tp: 16 (over z, x).
Axes of the slice: x: 4, y: 4, z: 4, core: 2. Of those that a mesh axis runs over, the one named last changes fastest.
Arguments:
- neighbour_ids: int32 [256, 128], replicated, may hold values from 0 to 15999
- neighbour_shard: int32 [256, 128, 1], replicated, may hold values from 0 to 7; in each aligned block of 4096 rows (0 to 4095, 4096 to 8191, ..., all dimensions but the last counted through in order) at most 1024 rows name the same one
- neighbour_count: int32 [64], replicated, may hold values from 1 to 4
- slot_beam: int32 [64], replicated, may hold values from 0 to 63, each once
- prefix_length: int32 [64], P('grp'), may hold values from 2 to 512
- embed_table: bfloat16 [128000, 2048], P('grp', 'tp')
- encoder_gain: float32 [2048], replicated, may hold values from 0.1 to 1.9
- hidden_in: bfloat16 [64, 8192], P('grp'), may hold values from -6 to 6
- decoder_gain: float32 [8192], replicated, may hold values from 0.1 to 1.9
- fresh_projections: bfloat16 [64, 3, 4096], P('grp', None, 'tp')
- cached_pairs: bfloat16 [64, 2, 512, 4096], P('grp', None, None, 'tp')
- w_self_out: bfloat16 [4096, 8192], P('tp'), may hold values from -0.375 to 0.375
- w_query: bfloat16 [8192, 4096], P(None, 'tp')
- w_pairs: bfloat16 [2048, 2, 4096], P(None, None, 'tp')
- w_cross_out: bfloat16 [4096, 8192], P('tp'), may hold values from -0.375 to 0.375
Outputs:
- self_delta: bfloat16 [64, 8192], P('grp')
- cross_delta: bfloat16 [64, 8192], P('grp')
The draws below stay inside these ranges and needn't reach their ends.
Inputs may be any that keep to these rules, and one draw needn't show every extreme that they name: `neighbour_shard`: in each aligned block of 4096 rows (slots in order, positions within a slot; block g holds the neighbours of beams 8g to 8g+7), at most 1024 rows name any one shard, a bound that some block reaches.
All inputs are finite; a program needn't handle non-finite values.
Results may differ from the reference program's by a relative error of at most 0.012.
The reference program's roundings to bfloat16 on the way count: a program that leaves them out, or rounds other values in their place, can miss the bound.
Values may be sent and summed in bfloat16 or wider, within the bound.
A program may use at most 128 MiB of HBM per device.

```python
import math
import jax
import jax.numpy as jnp
import numpy as np
from jax import lax

D = 8192
HEADS = 32
HD = 128
DE = 2048
VOCAB = 128000
NLEN = 128
KMAX = 4
CACHE = 512
BEAM_GRP = 8
BEAMS = 64
SLOTS = 256
VOCAB_SHARD = 16000
ROWS_CAP = 1024
N_GRP = 8


def shared_query(key):
    return jax.random.normal(jax.random.fold_in(key, 102), (BEAMS, HEADS, HD), dtype=jnp.float32)


def draw_prefix_length(key, part):
    key = jax.random.fold_in(key, 5)
    first_key, second_key = jax.random.split(key)
    lengths = jax.random.randint(first_key, (BEAMS,), 2, CACHE + 1, dtype=jnp.int32)
    chosen = jax.random.randint(second_key, (), 0, BEAMS, dtype=jnp.int32)
    return jnp.where(jnp.arange(BEAMS, dtype=jnp.int32) == chosen, CACHE, lengths).astype(jnp.int32)


def draw_embed_table(key, part):
    key = jax.random.fold_in(key, 1)
    first_key = jax.random.fold_in(key, 0)
    column_scale = 0.4 * jnp.power(10.0, jnp.arange(DE, dtype=jnp.float32) / DE)
    values = jax.random.normal(first_key, (VOCAB, DE), dtype=jnp.float32)
    return (values * column_scale[None, :]).astype(jnp.bfloat16)


def draw_fresh_projections(key, part):
    base = shared_query(key)
    key = jax.random.fold_in(key, 2)
    others = jax.random.normal(key, (BEAMS, 2, HEADS * HD), dtype=jnp.float32)
    queries = base
    return jnp.concatenate([queries.reshape(BEAMS, 1, HEADS * HD), others], axis=1).astype(jnp.bfloat16)


def draw_cached_pairs(key, part):
    key = jax.random.fold_in(key, 3)
    values = jax.random.normal(key, (BEAMS, 2, CACHE, HEADS, HD), dtype=jnp.float32)
    return values.reshape(BEAMS, 2, CACHE, HEADS * HD).astype(jnp.bfloat16)


def draw_w_query(key, part):
    key = jax.random.fold_in(key, 4)
    first_key = jax.random.fold_in(key, 0)
    values = jax.random.normal(first_key, (D, HEADS, HD), dtype=jnp.float32) / math.sqrt(D)
    return values.reshape(D, HEADS * HD).astype(jnp.bfloat16)


def draw_w_pairs(key, part):
    key = jax.random.fold_in(key, 6)
    first_key = jax.random.fold_in(key, 0)
    values = jax.random.normal(first_key, (DE, 2, HEADS, HD), dtype=jnp.float32) / math.sqrt(DE)
    return values.reshape(DE, 2, HEADS * HD).astype(jnp.bfloat16)


def with_ends(drawn, own_key, smallest, high):
    dims = drawn.shape
    place = [jax.random.randint(jax.random.fold_in(own_key, axis), (), 0, dims[axis]) for axis in range(len(dims))]
    drawn = drawn.at[tuple(place)].set(smallest)
    longest = dims.index(max(dims))
    place[longest] = (place[longest] + 1) % dims[longest]
    return drawn.at[tuple(place)].set(high)


def levels(rng, shape, shards, least, largest):
    loudness, own = 1.0, jax.random.fold_in(rng, 6)
    for position, shards_of in shards:
        steps = jnp.exp(jax.random.uniform(jax.random.fold_in(own, position), (shards_of,), jnp.float32, least / len(shards), largest / len(shards)))
        loudness = loudness * jnp.repeat(steps, shape[position] // shards_of).reshape([-1 if axis == position else 1 for axis in range(len(shape))])
    return loudness


def rank_bounds(amount, slope):
    portions = [(1 << 20) // math.isqrt(rank ** slope) + 1 for rank in range(1, amount + 1)]
    scale = 1 + sum(portions) // (1 << 30)
    return np.cumsum(np.array([max(1, weight // scale) for weight in portions]))


def ranked_ids(own_key, shape, amount, slope):
    grid = rank_bounds(amount, slope)
    lot = jax.random.randint(jax.random.fold_in(own_key, 1), shape, 0, int(grid[amount - 1]))
    standing = jnp.searchsorted(jnp.asarray(grid, jnp.int32), lot, side="right")
    return jax.random.permutation(jax.random.fold_in(own_key, 2), amount)[standing].astype(jnp.int32)


def shared_out(own_key, own, number, rows, amount, top, limit, slope):
    sequence = jax.random.permutation(own_key, amount)
    heavy_load, usual = portions_of(amount, rows * top, limit, slope, True), portions_of(amount, rows * top, limit, slope, False)
    places = jnp.arange(amount)

    def named(sizes, turn):
        used = int((sizes > 0).sum())
        fixed = max(1, used // 4)
        shifted = fixed + (places - fixed + turn * (used - fixed)) % max(1, amount - fixed)
        return jnp.zeros((amount,), jnp.int32).at[sequence[jnp.where(places < fixed, places, shifted)]].set(jnp.asarray(sizes, jnp.int32))

    sizes = jnp.where(number % 4 == 0, named(heavy_load, number // 4), named(usual, number - number // 4 - 1))
    mixed = jax.random.permutation(jax.random.fold_in(own, 3), amount)
    donor, receiver = mixed[0:amount // 2 * 2:2], mixed[1:amount // 2 * 2:2]
    margin = jnp.minimum(sizes[donor] - 1, limit - sizes[receiver]) // 2
    margin = jnp.where((donor == sequence[0]) | (receiver == sequence[0]) | (sizes[receiver] == 0), 0, jnp.maximum(margin, 0))
    shifted = jax.random.randint(jax.random.fold_in(own, 4), (amount // 2,), 0, 1 << 20) % (margin + 1)
    sizes = sizes.at[donor].add(-shifted).at[receiver].add(shifted)
    members = jnp.searchsorted(jnp.cumsum(sizes), jnp.arange(rows * top), side="right").astype(jnp.int32)
    table = members.reshape(top, rows).T
    table = table[jax.random.permutation(jax.random.fold_in(own, 1), rows)]
    turn = jax.random.randint(jax.random.fold_in(own, 2), (rows, 1), 0, top)
    return jnp.take_along_axis(table, (jnp.arange(top)[None, :] + turn) % top, axis=1)


def portions_of(number_of, total, most, lean, full):
    weights = [(1 << 20) // math.isqrt(rank ** lean) + 1 for rank in range(1, number_of + 1)]
    largest = most if full else min(most, max(-(-total // number_of), total * weights[0] // sum(weights)))
    least = 1 if total - largest >= number_of - 1 else 0
    holding, surplus = [largest] + [least] * (number_of - 1), total - largest - least * (number_of - 1)
    while surplus > 0:
        free = [i for i in range(1, number_of) if holding[i] < largest] or [i for i in range(1, number_of) if holding[i] < most]
        mass, remaining = sum([weights[i] for i in free]), surplus
        for i in free:
            extra = min(most - holding[i], max(1, remaining * weights[i] // mass), surplus)
            holding[i] = holding[i] + extra
            surplus = surplus - extra
    return np.array(holding)


def bell_draw(stream_key, dims, scale, most, shards=(), kind=jnp.bfloat16):
    drawn = scale * jax.random.normal(stream_key, dims, jnp.float32)
    if shards:
        drawn = drawn * levels(stream_key, dims, shards, -0.22, 0.18)
    return jnp.clip(drawn, -most, most).astype(kind)


def setup_inputs(seed: int = 0) -> dict:
    keys = jax.random.split(jax.random.key(seed), 16)
    neighbour_ids = with_ends(ranked_ids(keys[0], (SLOTS, NLEN), VOCAB_SHARD, 2), jax.random.fold_in(keys[0], 3), 0, VOCAB_SHARD - 1).astype(jnp.int32)
    neighbour_shard_keys = jax.random.split(jax.random.fold_in(keys[1], 1), SLOTS * NLEN // (BEAM_GRP * KMAX * NLEN))
    neighbour_shard_turns = jax.random.permutation(jax.random.fold_in(keys[1], 3), SLOTS * NLEN // (BEAM_GRP * KMAX * NLEN))
    neighbour_shard = jax.vmap(lambda own, number: shared_out(jax.random.fold_in(keys[1], 2), own, number, BEAM_GRP * KMAX * NLEN, N_GRP, 1, ROWS_CAP, 2))(neighbour_shard_keys, neighbour_shard_turns).reshape((SLOTS, NLEN, 1))
    neighbour_count = with_ends(jax.random.randint(keys[2], (BEAMS,), 1, 5), jax.random.fold_in(keys[2], 1), 1, 4).astype(jnp.int32)
    slot_beam = jax.random.permutation(keys[3], BEAMS).astype(jnp.int32)
    prefix_length = draw_prefix_length(jax.random.fold_in(keys[15], 71), 0)
    embed_table = draw_embed_table(jax.random.fold_in(keys[15], 71), 0)
    encoder_gain = jnp.clip(1.0 + 0.18 * jax.random.normal(keys[6], (DE,), jnp.float32), 0.1, 1.9)
    hidden_in = bell_draw(keys[7], (BEAMS, D), 1.0, 6.0, ((0, 8),))
    decoder_gain = jnp.clip(1.0 + 0.18 * jax.random.normal(keys[8], (D,), jnp.float32), 0.1, 1.9)
    fresh_projections = draw_fresh_projections(jax.random.fold_in(keys[15], 71), 0)
    cached_pairs = draw_cached_pairs(jax.random.fold_in(keys[15], 71), 0)
    w_self_out = bell_draw(keys[11], (HEADS * HD, D), (HEADS * HD // 16) ** -0.5, 0.375, ((0, 16),))
    w_query = draw_w_query(jax.random.fold_in(keys[15], 71), 0)
    w_pairs = draw_w_pairs(jax.random.fold_in(keys[15], 71), 0)
    w_cross_out = bell_draw(keys[14], (HEADS * HD, D), (HEADS * HD // 16) ** -0.5, 0.375, ((0, 16),))
    return {"neighbour_ids": neighbour_ids, "neighbour_shard": neighbour_shard, "neighbour_count": neighbour_count, "slot_beam": slot_beam, "prefix_length": prefix_length, "embed_table": embed_table, "encoder_gain": encoder_gain, "hidden_in": hidden_in, "decoder_gain": decoder_gain, "fresh_projections": fresh_projections, "cached_pairs": cached_pairs, "w_self_out": w_self_out, "w_query": w_query, "w_pairs": w_pairs, "w_cross_out": w_cross_out}


epsilon = 1e-05

def softmax_rows(scores, live_mask):
    masked = jnp.where(live_mask, scores, -jnp.inf)
    maximum = lax.optimization_barrier(jnp.max(masked, axis=-1, keepdims=True))
    raised = jnp.exp(masked - maximum)
    return raised / lax.optimization_barrier(jnp.sum(raised, axis=-1, keepdims=True))

def reference(neighbour_ids, neighbour_shard, neighbour_count, slot_beam, prefix_length, embed_table, encoder_gain, hidden_in, decoder_gain, fresh_projections, cached_pairs, w_self_out, w_query, w_pairs, w_cross_out):
    inverse_root = 1.0 / math.sqrt(HD)
    full_ids = (neighbour_shard.reshape(SLOTS, NLEN) * VOCAB_SHARD + neighbour_ids).astype(jnp.int32)
    fresh_rows = fresh_projections.astype(jnp.float32).reshape(BEAMS, 3, HEADS, HD)
    cached = cached_pairs.astype(jnp.float32).reshape(BEAMS, 2, CACHE, HEADS, HD)
    old_scores = jnp.einsum('bhd,bphd->bhp', fresh_rows[:, 0], cached[:, 0]) * inverse_root
    new_scores = jnp.einsum('bhd,bhd->bh', fresh_rows[:, 0], fresh_rows[:, 1]) * inverse_root
    positions = jnp.arange(CACHE, dtype=jnp.int32)
    live_old = jnp.broadcast_to(positions[None, None, :] < prefix_length[:, None, None], old_scores.shape)
    live_mask = jnp.concatenate([live_old, jnp.ones(new_scores.shape + (1,), dtype=bool)], axis=-1)
    weights = softmax_rows(jnp.concatenate([old_scores, new_scores[..., None]], axis=-1), live_mask)
    weights = lax.optimization_barrier(weights.astype(jnp.bfloat16)).astype(jnp.float32)
    attended = jnp.einsum('bhp,bphd->bhd', weights[..., :CACHE], cached[:, 1]) + weights[..., CACHE:] * fresh_rows[:, 2]
    attended = attended.astype(jnp.bfloat16).reshape(BEAMS, HEADS * HD)
    self_full = jnp.dot(attended, w_self_out, preferred_element_type=jnp.float32)
    residual = hidden_in.astype(jnp.float32) + self_full
    normed = (residual * lax.rsqrt(lax.optimization_barrier(jnp.mean(residual * residual, axis=-1, keepdims=True)) + epsilon) * decoder_gain).astype(jnp.bfloat16)
    cross_query = jnp.dot(normed, w_query, preferred_element_type=jnp.float32).astype(jnp.bfloat16).reshape(BEAMS, HEADS, HD)
    pair_matrix = w_pairs.reshape(DE, 2 * HEADS * HD)
    tokens = jnp.arange(KMAX * NLEN, dtype=jnp.int32)

    def one_beam(beam_entry):
        beam_number, query_row = beam_entry
        token_rows = lax.dynamic_slice_in_dim(full_ids, (beam_number * KMAX).astype(jnp.int32), KMAX, 0).reshape(KMAX * NLEN)
        looked = jnp.take(embed_table, token_rows, axis=0).astype(jnp.float32)
        encoded = (looked * lax.rsqrt(lax.optimization_barrier(jnp.mean(looked * looked, axis=-1, keepdims=True)) + epsilon) * encoder_gain).astype(jnp.bfloat16)
        cross_pairs = jnp.dot(encoded, pair_matrix, preferred_element_type=jnp.float32).astype(jnp.bfloat16)
        cross_pairs = lax.optimization_barrier(cross_pairs).astype(jnp.float32).reshape(KMAX * NLEN, 2, HEADS, HD)
        live_count = neighbour_count[beam_number]
        scores = jnp.einsum('hd,thd->ht', query_row.astype(jnp.float32), cross_pairs[:, 0]) * inverse_root
        cross_weights = softmax_rows(scores, (tokens < live_count * NLEN)[None, :])
        cross_weights = lax.optimization_barrier(cross_weights.astype(jnp.bfloat16)).astype(jnp.float32)
        return jnp.einsum('ht,thd->hd', cross_weights, cross_pairs[:, 1]).astype(jnp.bfloat16)
    cross_attended = lax.map(one_beam, (slot_beam, cross_query)).reshape(BEAMS, HEADS * HD)
    cross_full = jnp.dot(cross_attended, w_cross_out, preferred_element_type=jnp.float32)
    return (self_full.astype(jnp.bfloat16), cross_full.astype(jnp.bfloat16))
```

```python
import functools
import math

import jax
import jax.numpy as jnp
from jax import lax
from jax.experimental import pallas as pl
from jax.experimental.pallas import tpu as pltpu
from jax.sharding import PartitionSpec as P

MESH = pl.DeviceIdType.MESH
DMA = pltpu.SemaphoreType.DMA
VMEM = pl.BlockSpec(memory_space=pltpu.VMEM)
SMEM = pl.BlockSpec(memory_space=pltpu.SMEM)
ANY = pl.BlockSpec(memory_space=pl.ANY)

HD = 128
DE = 2048
NLEN = 128
KMAX = 4
CACHE = 512
CAP = 1024
GROUPS = 8
LANES = 16
ROOT = 1.0 / math.sqrt(HD)
epsilon = 1e-05
f32 = jnp.float32
bf16 = jnp.bfloat16
BIG = 56 * 2**20


def params(cid=None):
    if cid is None:
        return pltpu.CompilerParams(vmem_limit_bytes=BIG)
    return pltpu.CompilerParams(collective_id=cid, has_side_effects=True, vmem_limit_bytes=BIG)


def remote(src, dst, send, recv, where):
    return pltpu.make_async_remote_copy(
        src_ref=src, dst_ref=dst, send_sem=send, recv_sem=recv, device_id=where, device_id_type=MESH
    )


def greet(peers):
    barrier = pltpu.get_barrier_semaphore()
    for peer in peers:
        pl.semaphore_signal(barrier, inc=1, device_id=peer, device_id_type=MESH)
    pl.semaphore_wait(barrier, len(peers))


def prepare(ids, shards, counts, me):
    slots = jnp.arange(ids.shape[0], dtype=jnp.int32)
    alive = (slots % KMAX) < jnp.repeat(counts, KMAX)
    upper = jnp.triu(jnp.ones((NLEN, NLEN), bf16))
    chunks = ids.shape[0] // GROUPS
    strict = jnp.triu(jnp.ones((chunks, chunks), bf16), 1)

    def ranks(mask):
        inner = jnp.dot(mask.astype(bf16), upper, preferred_element_type=f32)
        before = jnp.dot(inner[..., -1].astype(bf16), strict, preferred_element_type=f32)
        return (inner + before[..., None]).astype(jnp.int32) - 1

    mine = ((shards == me) & alive[:, None]).reshape(GROUPS, chunks, NLEN)
    rank = ranks(mine)
    high, low = rank // 32, rank % 32
    small = jnp.arange(32, dtype=jnp.int32)
    rows = chunks * NLEN
    first = ((high[..., None] == small) & mine[..., None]).astype(bf16).reshape(GROUPS, rows, 32)
    second = low[..., None] == small
    ids3 = ids.reshape(GROUPS, chunks, NLEN)
    parts = jnp.concatenate(
        [
            jnp.where(second, (ids3 // 128)[..., None], 0),
            jnp.where(second, (ids3 % 128)[..., None], 0),
        ],
        axis=-1,
    ).astype(bf16)
    both = jnp.einsum(
        "gra,grb->gab", first, parts.reshape(GROUPS, rows, 64), preferred_element_type=f32
    )
    wanted = (both[..., :32] * 128.0 + both[..., 32:]).astype(jnp.int32).reshape(GROUPS * CAP)
    filled = jnp.sum(mine.astype(jnp.int32), axis=(1, 2))
    own_shards = lax.dynamic_slice_in_dim(shards, me * chunks, chunks)
    own_alive = lax.dynamic_slice_in_dim(alive, me * chunks, chunks)
    holder = jnp.arange(GROUPS, dtype=jnp.int32)[:, None, None]
    named = (own_shards[None] == holder) & own_alive[None, :, None]
    place = jnp.sum(jnp.where(named, ranks(named) + holder * CAP, 0), axis=0).reshape(rows)
    return wanted, filled, place


def look_kernel(wanted, filled, table, out, wide, found):
    step = 1600

    def widen(i, c):
        at = pl.ds(pl.multiple_of(i * step, step), step)
        wide[at, :] = table[at, :].astype(f32)
        return c

    lax.fori_loop(0, table.shape[0] // step, widen, 0)

    def block(g, c):
        base = g * CAP

        def sixteen(k, c):
            for u in range(16):
                found[k * 16 + u, :] = wide[wanted[base + k * 16 + u], :]
            return c

        lax.fori_loop(0, jnp.maximum((filled[g] + 15) // 16, 1), sixteen, 0)
        out[g] = found[...].astype(bf16)
        return c

    lax.fori_loop(0, GROUPS, block, 0)


def look(wanted, filled, table):
    return pl.pallas_call(
        look_kernel,
        out_shape=jax.ShapeDtypeStruct((GROUPS, CAP, table.shape[1]), bf16),
        in_specs=[SMEM, SMEM, VMEM],
        out_specs=VMEM,
        scratch_shapes=[pltpu.VMEM(table.shape, f32), pltpu.VMEM((CAP, table.shape[1]), f32)],
        compiler_params=params(),
        name="look",
    )(wanted, filled, table)


def place_kernel(place, got, out, wide, found):
    for g in range(GROUPS):
        wide[pl.ds(g * CAP, CAP), :] = got[g].astype(f32)

    def pair(p, c):
        base = p * 1024

        def sixteen(k, c):
            for u in range(16):
                found[k * 16 + u, :] = wide[place[base + k * 16 + u], :]
            return c

        lax.fori_loop(0, 64, sixteen, 0)
        out[p] = found[...].astype(bf16)
        return c

    lax.fori_loop(0, 4, pair, 0)


def put_in_place(place, got):
    return pl.pallas_call(
        place_kernel,
        out_shape=jax.ShapeDtypeStruct((4, 1024, got.shape[2]), bf16),
        in_specs=[SMEM, VMEM],
        out_specs=VMEM,
        scratch_shapes=[
            pltpu.VMEM((GROUPS * CAP, got.shape[2]), f32),
            pltpu.VMEM((1024, got.shape[2]), f32),
        ],
        compiler_params=params(),
        name="put_in_place",
    )(place, got)


class Ring:
    def __init__(self, w, base, out, first, send, recv, fsend, frecv):
        g, t = lax.axis_index("grp"), lax.axis_index("tp")
        core = lax.rem(g, 2)
        self.sibling = {"grp": g + 1 - 2 * core}
        z, x = t // 4, lax.rem(t, 4)
        right, left = lax.rem(x + 1, 4), lax.rem(x + 3, 4)
        far = lax.rem(x + 2, 4)
        self.fsend, self.frecv, self.out = fsend, frecv, out
        self.half = pl.ds(pl.multiple_of(first + core * 512, 512), 512)
        src = w.at[pl.ds(pl.multiple_of(base + core * 512, 512), 512)]
        dst = out.at[x, self.half]
        to_right, to_left = {"tp": z * 4 + right}, {"tp": z * 4 + left}
        self.near = [
            remote(src, dst, send.at[0], recv.at[0], to_right),
            remote(src, dst, send.at[1], recv.at[1], to_left),
        ]
        onward = lax.rem(x + 1 + 2 * core, 4)
        behind = lax.rem(x + 3 + 2 * core, 4)
        self.first_in = remote(src, out.at[behind, self.half], send.at[0], recv.at[core], to_right)
        self.second_in = remote(src, out.at[onward, self.half], send.at[0], recv.at[1 - core], to_right)
        moved = out.at[behind, self.half]
        self.relay = remote(moved, moved, send.at[2], recv.at[2], {"tp": z * 4 + onward})
        self.relay_in = remote(
            moved, out.at[far, self.half], send.at[2], recv.at[2], {"tp": z * 4 + onward}
        )
        self.hands = []
        for k, shard in enumerate((behind, onward, far)):
            piece = out.at[shard, self.half]
            self.hands.append(remote(piece, piece, fsend.at[k], frecv.at[k], self.sibling))

    def start(self):
        for copy in self.near:
            copy.start()

    def service(self):
        self.first_in.wait_recv()
        self.relay.start()
        self.hands[0].start()

    def service_more(self):
        self.second_in.wait_recv()
        self.hands[1].start()

    def service_last(self):
        self.relay_in.wait_recv()
        self.hands[2].start()

    def finish(self):
        for copy in self.near:
            copy.wait_send()
        self.relay.wait_send()
        for copy in self.hands:
            copy.wait()


def head_rows(row):
    rows = lax.broadcasted_iota(jnp.int32, (8, 2 * HD), 0)
    lanes = lax.broadcasted_iota(jnp.int32, (8, 2 * HD), 1)
    return jnp.where(lanes // HD == rows, jnp.broadcast_to(row, (8, 2 * HD)), 0.0)


def head_pick(full):
    rows = lax.broadcasted_iota(jnp.int32, (8, 2 * HD), 0)
    lanes = lax.broadcasted_iota(jnp.int32, (8, 2 * HD), 1)
    return jnp.sum(jnp.where(lanes // HD == rows, full, 0.0), axis=0, keepdims=True)


def dot(a, b):
    return jnp.dot(a, b, preferred_element_type=f32)


def dot_t(a, b):
    return lax.dot_general(a, b, (((1,), (1,)), ((), ())), preferred_element_type=f32)


def self_kernel(
    rows, fresh, prefix, cached, w_self, hidden, gain, w_query, w,
    got, gathered, delta, query,
    vc, vs, vq, attended, part, red, full,
    lsem, ysend, yrecv, psend, precv, asend, arecv, wsend, wrecv, fsend, frecv,
):
    g, t = lax.axis_index("grp"), lax.axis_index("tp")
    x = lax.rem(t, 4)
    loads = [
        pltpu.make_async_copy(cached, vc, lsem.at[0]),
        pltpu.make_async_copy(w_self, vs, lsem.at[1]),
        pltpu.make_async_copy(w_query, vq, lsem.at[2]),
        pltpu.make_async_copy(rows.at[g], got.at[g], lsem.at[3]),
        pltpu.make_async_copy(w.at[pl.ds(0, 1024)], gathered.at[x], lsem.at[4]),
    ]
    for copy in loads:
        copy.start()
    groups = [lax.rem(g + d, GROUPS) for d in range(1, GROUPS)]
    lanes = [lax.rem(t + d, LANES) for d in range(1, LANES)]
    greet([{"grp": p} for p in groups] + [{"tp": p} for p in lanes])
    ring = Ring(w, 0, gathered, 0, wsend, wrecv, fsend, frecv)
    sends = []
    for k, p in enumerate(groups):
        copy = remote(rows.at[p], got.at[g], ysend.at[k], yrecv.at[k], {"grp": p})
        copy.start()
        sends.append(copy)
    ring.start()

    loads[0].wait()
    positions = lax.broadcasted_iota(jnp.int32, (8, CACHE), 1)
    for b in range(8):
        spread = head_rows(fresh[0, pl.ds(b, 1), :])
        scores = dot_t(spread.astype(bf16), vc[b, 0]) * ROOT
        fresh_score = jnp.sum(spread * fresh[1, pl.ds(b, 1), :], axis=1, keepdims=True) * ROOT
        live = positions < prefix[b]
        top = jnp.maximum(
            jnp.max(jnp.where(live, scores, -jnp.inf), axis=1, keepdims=True), fresh_score
        )
        raised = jnp.where(live, jnp.exp(scores - top), 0.0)
        fresh_raised = jnp.exp(fresh_score - top)
        total = jnp.sum(raised, axis=1, keepdims=True) + fresh_raised
        weights = (raised / total).astype(bf16)
        fresh_weight = (fresh_raised / total).astype(bf16).astype(f32)
        mixed = dot(weights, vc[b, 1]) + fresh_weight * fresh[2, pl.ds(b, 1), :]
        attended[pl.ds(b, 1), :] = head_pick(mixed)
    ring.service()
    loads[1].wait()
    held = attended[...].astype(bf16)
    reduce = []
    for d in range(1, LANES + 1):
        p = lax.rem(t + d, LANES)
        part[p] = dot(held, vs[:, pl.ds(pl.multiple_of(p * 512, 512), 512)])
        if d < LANES:
            copy = remote(part.at[p], red.at[t], psend.at[d - 1], precv.at[d - 1], {"tp": p})
            copy.start()
            reduce.append(copy)
    ring.service_more()
    total = part[t]
    for d, copy in enumerate(reduce):
        copy.wait_recv()
        total = total + red[lax.rem(t + LANES - 1 - d, LANES)]
    full[t] = total
    share = []
    for d, p in enumerate(lanes):
        copy = remote(full.at[t], full.at[t], asend.at[d], arecv.at[d], {"tp": p})
        copy.start()
        share.append(copy)
    ring.service_last()
    for d, copy in enumerate(share):
        copy.wait_recv()
    squares = jnp.zeros((8, 512), f32)
    for c in range(LANES):
        at = pl.ds(c * 512, 512)
        summed = full[c]
        delta[:, at] = summed.astype(bf16)
        r = hidden[:, at].astype(f32) + summed
        squares = squares + r * r
    scale = lax.rsqrt(jnp.sum(squares, axis=1, keepdims=True) / (LANES * 512) + epsilon)
    loads[2].wait()
    out = jnp.zeros((8, 2 * HD), f32)
    for c in range(LANES):
        at = pl.ds(c * 512, 512)
        r = hidden[:, at].astype(f32) + full[c]
        normed = (r * scale * gain[:, at]).astype(bf16)
        out = out + dot(normed, vq[at, :])
    query[...] = out.astype(bf16).astype(f32)
    for copy in reduce:
        copy.wait_send()
    for copy in share:
        copy.wait_send()
    for copy in sends:
        copy.wait()
    ring.finish()
    loads[3].wait()
    loads[4].wait()


def self_part(rows, fresh, prefix, cached, w_self, hidden, gain, w_query, w):
    return pl.pallas_call(
        self_kernel,
        out_shape=(
            jax.ShapeDtypeStruct(rows.shape, bf16),
            jax.ShapeDtypeStruct((4, 1024, 512), bf16),
            jax.ShapeDtypeStruct(hidden.shape, bf16),
            jax.ShapeDtypeStruct((8, 2 * HD), f32),
        ),
        in_specs=[ANY, VMEM, SMEM, ANY, ANY, VMEM, VMEM, ANY, ANY],
        out_specs=(ANY, ANY, VMEM, VMEM),
        scratch_shapes=[
            pltpu.VMEM(cached.shape, bf16),
            pltpu.VMEM(w_self.shape, bf16),
            pltpu.VMEM(w_query.shape, bf16),
            pltpu.VMEM((8, 2 * HD), f32),
            pltpu.VMEM((LANES, 8, 512), f32),
            pltpu.VMEM((LANES, 8, 512), f32),
            pltpu.VMEM((LANES, 8, 512), f32),
            DMA((5,)),
            DMA((7,)),
            DMA((7,)),
            DMA((15,)),
            DMA((15,)),
            DMA((15,)),
            DMA((15,)),
            DMA((3,)),
            DMA((3,)),
            DMA((3,)),
            DMA((3,)),
        ],
        compiler_params=params(0),
        name="self_part",
    )(rows, fresh, prefix, cached, w_self, hidden, gain, w_query, w)


def cross_kernel(
    rows, query, beams, slots, counts, gain, gathered, w, w_cross,
    delta,
    zb, vw, vx, enc, pairs, qb, asent, ab, part, red, full,
    lsem, xsend, xrecv, zsend, zrecv, qsend, qrecv, bsend, brecv,
    psend, precv, gsend, grecv, wsend, wrecv, fsend, frecv,
):
    g, t = lax.axis_index("grp"), lax.axis_index("tp")
    z, x = t // 4, lax.rem(t, 4)
    loads = [
        pltpu.make_async_copy(gathered, vw.at[:, pl.ds(0, 1024)], lsem.at[0]),
        pltpu.make_async_copy(w.at[pl.ds(1024, 1024)], vw.at[x, pl.ds(1024, 1024)], lsem.at[1]),
        pltpu.make_async_copy(w_cross, vx, lsem.at[2]),
        pltpu.make_async_copy(query, qb.at[g, x], lsem.at[3]),
    ]
    own = [
        pltpu.make_async_copy(
            rows.at[x, pl.ds(c * 256, 256)], zb.at[z, c, x], lsem.at[4 + c]
        )
        for c in range(4)
    ]
    for copy in loads + own:
        copy.start()
    lanes = [lax.rem(t + d, LANES) for d in range(1, LANES)]
    cloud = []
    for dg in range(GROUPS):
        for dx in range(4):
            if dg or dx:
                cloud.append((lax.rem(g + dg, GROUPS), lax.rem(x + dx, 4), dg, dx))
    greet(
        [{"tp": p} for p in lanes]
        + [{"grp": pg, "tp": z * 4 + px} for pg, px, dg, _ in cloud if dg]
    )
    ring = Ring(w, 1024, vw, 1024, wsend, wrecv, fsend, frecv)
    xs = []
    for c in range(4):
        line = []
        for d in range(1, 4):
            px = lax.rem(x + d, 4)
            copy = remote(
                rows.at[px, pl.ds(c * 256, 256)], zb.at[z, c, x],
                xsend.at[c, d - 1], xrecv.at[c, d - 1], {"tp": z * 4 + px},
            )
            copy.start()
            line.append(copy)
        xs.append(line)
    ring.start()
    asks = []
    for k, (pg, px, dg, dx) in enumerate(cloud):
        copy = remote(
            query, qb.at[g, x], qsend.at[k], qrecv.at[k], {"grp": pg, "tp": z * 4 + px}
        )
        copy.start()
        asks.append(copy)
    up, down = lax.rem(z + 1, 4), lax.rem(z + 3, 4)
    ups, downs, relays = [], [], []
    for c in range(4):
        own[c].wait()
        for copy in xs[c]:
            copy.wait_recv()
        mine = zb.at[z, c]
        ups.append(remote(mine, mine, zsend.at[c, 0], zrecv.at[c, 0], {"tp": up * 4 + x}))
        downs.append(remote(mine, mine, zsend.at[c, 1], zrecv.at[c, 1], {"tp": down * 4 + x}))
        ups[c].start()
        downs[c].start()
    ring.service()
    for c in range(4):
        if c % 2 == 0:
            ups[c].wait_recv()
            piece, to = zb.at[down, c], up
        else:
            downs[c].wait_recv()
            piece, to = zb.at[up, c], down
        relays.append(remote(piece, piece, zsend.at[c, 2], zrecv.at[c, 2], {"tp": to * 4 + x}))
        relays[c].start()
        if c == 0:
            ring.service_more()
        if c == 1:
            ring.service_last()
    for copy in loads:
        copy.wait()
    ring.finish()
    for copy in asks:
        copy.wait()
    for c in range(4):
        if c % 2 == 0:
            downs[c].wait_recv()
        else:
            ups[c].wait_recv()
        relays[c].wait_recv()
        squares = jnp.zeros((256, HD), f32)
        for p in range(LANES):
            piece = zb[p // 4, c, p % 4].astype(f32)
            squares = squares + piece * piece
        scale = lax.rsqrt(jnp.sum(squares, axis=1, keepdims=True) / DE + epsilon)
        for p in range(LANES):
            at = pl.ds(p * HD, HD)
            enc[:, at] = (zb[p // 4, c, p % 4].astype(f32) * scale * gain[:, at]).astype(bf16)

        def project(k, carry):
            pairs[c, k] = dot(enc[...], vw[k]).astype(bf16)
            return carry

        lax.fori_loop(0, 4, project, 0)

    first = g * 8 + x * 2
    numbers = lax.broadcasted_iota(jnp.int32, (8, 64), 0) + first
    chosen = (numbers == beams[...]).astype(bf16)
    tokens = lax.broadcasted_iota(jnp.int32, (8, KMAX * NLEN), 1)
    sides = lax.broadcasted_iota(jnp.int32, (8, 2 * HD), 0)
    for k in range(4):
        asked = dot(chosen, qb[:, k].reshape(64, 2 * HD).astype(bf16))
        answers = []
        for i in range(2):
            spread = head_rows(asked[i : i + 1, :]).astype(bf16)
            scores = jnp.concatenate(
                [dot_t(spread, pairs[2 * i + h, k, :, : 2 * HD]) for h in range(2)], axis=1
            )
            live = tokens < counts[first + i] * NLEN
            scores = jnp.where(live, scores * ROOT, -jnp.inf)
            raised = jnp.exp(scores - jnp.max(scores, axis=1, keepdims=True))
            weights = (raised / jnp.sum(raised, axis=1, keepdims=True)).astype(bf16)
            mixed = dot(weights[:, :256], pairs[2 * i, k, :, 2 * HD :])
            mixed = mixed + dot(weights[:, 256:], pairs[2 * i + 1, k, :, 2 * HD :])
            answers.append(head_pick(mixed))
        asent[k] = jnp.where(
            sides == 0, answers[0], jnp.where(sides == 1, answers[1], 0.0)
        ).astype(bf16).astype(f32)
    ab[g, x] = asent[x]
    replies = []
    for k, (pg, px, dg, dx) in enumerate(cloud):
        copy = remote(
            asent.at[px], ab.at[g, x], bsend.at[k], brecv.at[k], {"grp": pg, "tp": z * 4 + px}
        )
        copy.start()
        replies.append(copy)
    for copy in replies:
        copy.wait_recv()
    spots = lax.broadcasted_iota(jnp.int32, (8, 256), 1)
    inner = lax.rem(spots, 8)
    owner = (spots // 32) * 8 + lax.rem(spots // 8, 4) * 2 + inner
    picks = ((owner == slots[...]) & (inner < 2)).astype(bf16)
    held = dot(picks, ab[...].reshape(256, 2 * HD).astype(bf16)).astype(bf16)
    reduce = []
    for d in range(1, LANES + 1):
        p = lax.rem(t + d, LANES)
        part[p] = dot(held, vx[:, pl.ds(pl.multiple_of(p * 512, 512), 512)])
        if d < LANES:
            copy = remote(part.at[p], red.at[t], psend.at[d - 1], precv.at[d - 1], {"tp": p})
            copy.start()
            reduce.append(copy)
    total = part[t]
    for d, copy in enumerate(reduce):
        copy.wait_recv()
        total = total + red[lax.rem(t + LANES - 1 - d, LANES)]
    full[t] = total
    share = []
    for d, p in enumerate(lanes):
        copy = remote(full.at[t], full.at[t], gsend.at[d], grecv.at[d], {"tp": p})
        copy.start()
        share.append(copy)
    for copy in share:
        copy.wait_recv()
    for c in range(LANES):
        delta[:, pl.ds(c * 512, 512)] = full[c].astype(bf16)
    for line in xs:
        for copy in line:
            copy.wait_send()
    for copy in ups + downs + relays + replies + reduce + share:
        copy.wait_send()


def cross_part(rows, query, beams, slots, counts, gain, gathered, w, w_cross, width):
    return pl.pallas_call(
        cross_kernel,
        out_shape=jax.ShapeDtypeStruct((8, width), bf16),
        in_specs=[ANY, VMEM, VMEM, VMEM, SMEM, VMEM, ANY, ANY, ANY],
        out_specs=VMEM,
        scratch_shapes=[
            pltpu.VMEM((4, 4, 4, 256, HD), bf16),
            pltpu.VMEM((4, DE, 512), bf16),
            pltpu.VMEM(w_cross.shape, bf16),
            pltpu.VMEM((256, DE), bf16),
            pltpu.VMEM((4, 4, 256, 512), bf16),
            pltpu.VMEM((GROUPS, 4, 8, 2 * HD), f32),
            pltpu.VMEM((4, 8, 2 * HD), f32),
            pltpu.VMEM((GROUPS, 4, 8, 2 * HD), f32),
            pltpu.VMEM((LANES, 8, 512), f32),
            pltpu.VMEM((LANES, 8, 512), f32),
            pltpu.VMEM((LANES, 8, 512), f32),
            DMA((8,)),
            DMA((4, 3)),
            DMA((4, 3)),
            DMA((4, 3)),
            DMA((4, 3)),
            DMA((31,)),
            DMA((31,)),
            DMA((31,)),
            DMA((31,)),
            DMA((15,)),
            DMA((15,)),
            DMA((15,)),
            DMA((15,)),
            DMA((3,)),
            DMA((3,)),
            DMA((3,)),
            DMA((3,)),
        ],
        compiler_params=params(1),
        name="cross_part",
    )(rows, query, beams, slots, counts, gain, gathered, w, w_cross)


def local(
    neighbour_ids,
    neighbour_shard,
    neighbour_count,
    slot_beam,
    prefix_length,
    embed_table,
    encoder_gain,
    hidden_in,
    decoder_gain,
    fresh_projections,
    cached_pairs,
    w_self_out,
    w_query,
    w_pairs,
    w_cross_out,
):
    me = lax.axis_index("grp")
    shards = neighbour_shard.reshape(neighbour_ids.shape)
    wanted, filled, place = prepare(neighbour_ids, shards, neighbour_count, me)
    rows = look(wanted, filled, embed_table)
    w = w_pairs.reshape(DE, 512)
    fresh = jnp.transpose(fresh_projections.astype(f32), (1, 0, 2))
    got, gathered, self_delta, query = self_part(
        rows, fresh, prefix_length, cached_pairs, w_self_out, hidden_in,
        decoder_gain[None, :], w_query, w,
    )
    placed = put_in_place(place, got)
    slots = lax.dynamic_slice_in_dim(slot_beam, me * 8, 8)
    cross_delta = cross_part(
        placed, query, slot_beam[None, :], slots[:, None], neighbour_count,
        encoder_gain[None, :], gathered, w, w_cross_out, hidden_in.shape[1],
    )
    return self_delta, cross_delta


def solution(mesh):
    placed = (
        P(),
        P(),
        P(),
        P(),
        P("grp"),
        P("grp", "tp"),
        P(),
        P("grp", None),
        P(),
        P("grp", None, "tp"),
        P("grp", None, None, "tp"),
        P("tp", None),
        P(None, "tp"),
        P(None, None, "tp"),
        P("tp", None),
    )
    return jax.shard_map(
        local,
        mesh=mesh,
        in_specs=placed,
        out_specs=(P("grp", None), P("grp", None)),
        check_vma=False,
    )
```

```python
import math

import jax
import jax.numpy as jnp
from jax import lax
from jax.experimental import pallas as pl
from jax.experimental.pallas import tpu as pltpu
from jax.sharding import PartitionSpec as P

MESH = pl.DeviceIdType.MESH
DMA = pltpu.SemaphoreType.DMA
VMEM = pl.BlockSpec(memory_space=pltpu.VMEM)
SMEM = pl.BlockSpec(memory_space=pltpu.SMEM)
ANY = pl.BlockSpec(memory_space=pl.ANY)

HD = 128
DE = 2048
NLEN = 128
KMAX = 4
CACHE = 512
CAP = 1024
GROUPS = 8
LANES = 16
ROOT = 1.0 / math.sqrt(HD)
epsilon = 1e-05
f32 = jnp.float32
bf16 = jnp.bfloat16
BIG = 62 * 2**20


def params(cid=None):
    if cid is None:
        return pltpu.CompilerParams(vmem_limit_bytes=BIG)
    return pltpu.CompilerParams(collective_id=cid, has_side_effects=True, vmem_limit_bytes=BIG)


def remote(src, dst, send, recv, where):
    return pltpu.make_async_remote_copy(
        src_ref=src, dst_ref=dst, send_sem=send, recv_sem=recv, device_id=where, device_id_type=MESH
    )


def head_rows(row):
    rows = lax.broadcasted_iota(jnp.int32, (8, 2 * HD), 0)
    lanes = lax.broadcasted_iota(jnp.int32, (8, 2 * HD), 1)
    return jnp.where(lanes // HD == rows, jnp.broadcast_to(row, (8, 2 * HD)), 0.0)


def head_pick(full):
    rows = lax.broadcasted_iota(jnp.int32, (8, 2 * HD), 0)
    lanes = lax.broadcasted_iota(jnp.int32, (8, 2 * HD), 1)
    return jnp.sum(jnp.where(lanes // HD == rows, full, 0.0), axis=0, keepdims=True)


def dot(a, b):
    return jnp.dot(a, b, preferred_element_type=f32)


def dot_t(a, b):
    return lax.dot_general(a, b, (((1,), (1,)), ((), ())), preferred_element_type=f32)


def prep_kernel(ids, shards, counts, wanted, place):
    me = lax.axis_index("grp")
    rows = lax.broadcasted_iota(jnp.int32, (256, 1), 0)
    of_beam = (
        lax.broadcasted_iota(jnp.int32, (256, 64), 0) // KMAX
        == lax.broadcasted_iota(jnp.int32, (256, 64), 1)
    ).astype(bf16)
    held = dot(of_beam, jnp.broadcast_to(counts[...], (64, NLEN)).astype(bf16))
    alive = (rows % KMAX).astype(f32) < held
    upper = (
        lax.broadcasted_iota(jnp.int32, (NLEN, NLEN), 0)
        <= lax.broadcasted_iota(jnp.int32, (NLEN, NLEN), 1)
    ).astype(bf16)
    down = lax.broadcasted_iota(jnp.int32, (256, 256), 0)
    along = lax.broadcasted_iota(jnp.int32, (256, 256), 1)
    before = ((down // 32 == along // 32) & (along < down)).astype(bf16)
    ones = jnp.ones((NLEN, NLEN), bf16)

    def ranks(mask):
        mask = mask.astype(bf16)
        return dot(mask, upper) + dot(before, dot(mask, ones).astype(bf16)) - 1.0

    mine = (shards[...] == me) & alive
    rank = jnp.where(mine, ranks(mine), -1.0).astype(jnp.int32)
    high, low = rank >> 5, rank & 31
    high = jnp.where(mine, high, -1)
    id_high, id_low = (ids[...] >> 7).astype(f32), (ids[...] & 127).astype(f32)
    small = lax.broadcasted_iota(jnp.int32, (32, NLEN), 0)
    for g in range(GROUPS):
        left, right = [], []
        for i in range(32 * g, 32 * g + 32):
            left.append((small == high[i : i + 1]).astype(bf16))
            spot = small == low[i : i + 1]
            right.append(
                jnp.concatenate(
                    [
                        jnp.where(spot, id_high[i : i + 1], 0.0).astype(bf16),
                        jnp.where(spot, id_low[i : i + 1], 0.0).astype(bf16),
                    ],
                    axis=0,
                )
            )
        both = dot_t(jnp.concatenate(left, axis=1), jnp.concatenate(right, axis=1))
        wanted[g] = (both[:, :32] * 128.0 + both[:, 32:]).astype(jnp.int32)

    at = pl.ds(pl.multiple_of(me * 32, 32), 32)
    own = jnp.concatenate([shards[at, :]] * GROUPS, axis=0)
    beam = me * 8 + lax.broadcasted_iota(jnp.int32, (256, 64), 0) % 32 // KMAX
    of_own = (beam == lax.broadcasted_iota(jnp.int32, (256, 64), 1)).astype(bf16)
    own_held = dot(of_own, jnp.broadcast_to(counts[...], (64, NLEN)).astype(bf16))
    named = (own == rows // 32) & ((rows % KMAX).astype(f32) < own_held)
    spots = jnp.where(named, ranks(named) + (rows // 32 * CAP).astype(f32), 0.0).astype(jnp.int32)
    total = spots[0:32]
    for s in range(1, GROUPS):
        total = total + spots[32 * s : 32 * s + 32]
    place[...] = total


def prepare(ids, shards, counts):
    return pl.pallas_call(
        prep_kernel,
        out_shape=(
            jax.ShapeDtypeStruct((GROUPS, 32, 32), jnp.int32),
            jax.ShapeDtypeStruct((32, NLEN), jnp.int32),
        ),
        in_specs=[VMEM, VMEM, VMEM],
        out_specs=(VMEM, VMEM),
        compiler_params=params(),
        name="prep",
    )(ids, shards, counts)


class Ring:
    def __init__(self, out, here, peer, sems):
        g = lax.axis_index("grp")
        core = lax.rem(g, 2)
        send, recv, fsend, frecv = sems
        half = pl.ds(pl.multiple_of(core * 1024, 1024), 1024)
        right, left = lax.rem(here + 1, 4), lax.rem(here + 3, 4)
        onward, behind = lax.rem(here + 1 + 2 * core, 4), lax.rem(here + 3 + 2 * core, 4)
        mine, moved = out.at[here, half], out.at[behind, half]
        self.near = [
            remote(mine, mine, send.at[0], recv.at[0], peer(right)),
            remote(mine, mine, send.at[1], recv.at[1], peer(left)),
        ]
        self.first_in = remote(mine, moved, send.at[0], recv.at[core], peer(right))
        self.second_in = remote(
            mine, out.at[onward, half], send.at[0], recv.at[1 - core], peer(right)
        )
        self.relay = remote(moved, moved, send.at[2], recv.at[2], peer(onward))
        self.relay_in = remote(
            moved, out.at[lax.rem(here + 2, 4), half], send.at[2], recv.at[2], peer(onward)
        )
        self.hands = []
        for k, shard in enumerate((behind, onward, lax.rem(here + 2, 4))):
            piece = out.at[shard, half]
            self.hands.append(
                remote(piece, piece, fsend.at[k], frecv.at[k], {"grp": g + 1 - 2 * core})
            )

    def start(self):
        for copy in self.near:
            copy.start()

    def service(self):
        self.first_in.wait_recv()
        self.relay.start()
        self.hands[0].start()

    def service_more(self):
        self.second_in.wait_recv()
        self.hands[1].start()

    def service_last(self):
        self.relay_in.wait_recv()
        self.hands[2].start()

    def finish(self):
        for copy in self.near:
            copy.wait_send()
        self.relay.wait_send()
        for copy in self.hands:
            copy.wait()


class Spread:
    def __init__(self, held, weights, part, red, full, sems):
        self.held, self.weights, self.part, self.red, self.full = held, weights, part, red, full
        self.psend, self.precv, self.asend, self.arecv = sems
        self.t = lax.axis_index("tp")

    def start(self):
        self.reduce = []
        for d in range(1, LANES + 1):
            p = lax.rem(self.t + d, LANES)
            at = pl.ds(pl.multiple_of(p * 512, 512), 512)
            self.part[p] = dot(self.held, self.weights[:, at])
            if d < LANES:
                copy = remote(
                    self.part.at[p], self.red.at[self.t],
                    self.psend.at[d - 1], self.precv.at[d - 1], {"tp": p},
                )
                copy.start()
                self.reduce.append(copy)

    def share(self):
        total = self.part[self.t]
        for d, copy in enumerate(self.reduce):
            copy.wait_recv()
            total = total + self.red[lax.rem(self.t + LANES - 1 - d, LANES)]
        self.full[self.t] = total
        self.shared = []
        for d in range(1, LANES):
            mine = self.full.at[self.t]
            copy = remote(
                mine, mine, self.asend.at[d - 1], self.arecv.at[d - 1],
                {"tp": lax.rem(self.t + d, LANES)},
            )
            copy.start()
            self.shared.append(copy)

    def arrive(self):
        for copy in self.shared:
            copy.wait_recv()

    def finish(self):
        for copy in self.reduce + self.shared:
            copy.wait_send()


class Move:
    def __init__(self, placed, first, out, a, b, peer_a, peer_b, sems):
        self.asend, self.arecv, self.bsend, self.brecv, self.own = sems
        self.placed, self.first, self.out = placed, first, out
        self.a, self.b, self.peer_a, self.peer_b = a, b, peer_a, peer_b
        self.exchanged, self.ups, self.downs, self.relays, self.kept = {}, {}, {}, {}, {}

    def exchange(self, h):
        a, b = self.a, self.b
        line = []
        for d in (1, 3, 2):
            p = lax.rem(a + d, 4)
            copy = remote(
                self.placed.at[h, self.first + p], self.out.at[b, h, a],
                self.asend.at[h, d - 1], self.arecv.at[h, d - 1], self.peer_a(p),
            )
            copy.start()
            line.append(copy)
        self.exchanged[h] = line
        self.kept[h] = pltpu.make_async_copy(
            self.placed.at[h, self.first + a], self.out.at[b, h, a], self.own.at[h]
        )
        self.kept[h].start()

    def gather(self, h):
        self.kept[h].wait()
        for copy in self.exchanged[h]:
            copy.wait_recv()
        mine = self.out.at[self.b, h]
        up, down = lax.rem(self.b + 1, 4), lax.rem(self.b + 3, 4)
        self.ups[h] = remote(
            mine, mine, self.bsend.at[h, 0], self.brecv.at[h, 0], self.peer_b(up)
        )
        self.downs[h] = remote(
            mine, mine, self.bsend.at[h, 1], self.brecv.at[h, 1], self.peer_b(down)
        )
        self.ups[h].start()
        self.downs[h].start()

    def relay(self, h):
        up, down = lax.rem(self.b + 1, 4), lax.rem(self.b + 3, 4)
        if h % 2 == 0:
            self.ups[h].wait_recv()
            piece, to = self.out.at[down, h], up
        else:
            self.downs[h].wait_recv()
            piece, to = self.out.at[up, h], down
        self.relays[h] = remote(
            piece, piece, self.bsend.at[h, 2], self.brecv.at[h, 2], self.peer_b(to)
        )
        self.relays[h].start()

    def arrive(self, h):
        (self.downs if h % 2 == 0 else self.ups)[h].wait_recv()
        self.relays[h].wait_recv()

    def finish(self):
        for h in self.ups:
            for copy in self.exchanged[h]:
                copy.wait_send()
            for copy in (self.ups[h], self.downs[h], self.relays[h]):
                copy.wait_send()


def step_kernel(
    wanted, place, prefix, counts, fresh, beams, slots, hidden, gain, egain,
    table, cached, w_self, w_query, w, w_cross,
    delta, out,
    tbuf, wide, found, rows, got, wbuf, wx, wz, vc, vs, vq, attended,
    part, red, full, cpart, cred, cfull,
    placed, xb, zb, enc, pairs, qall, qsend_buf, qx, qz, answers, ab, aall,
    tsem, wsem, lsem, ysend, yrecv, rsems, csems, xw, zw, xm, zm,
    qgsend, qgrecv, qtsend, qtrecv, atsend, atrecv, agsend, agrecv,
):
    g, t = lax.axis_index("grp"), lax.axis_index("tp")
    z, x = t // 4, lax.rem(t, 4)
    groups = [lax.rem(g + d, GROUPS) for d in range(1, GROUPS)]
    lanes = [lax.rem(t + d, LANES) for d in range(1, LANES)]
    peers = [{"grp": p} for p in groups] + [{"tp": p} for p in lanes]
    barrier = pltpu.get_barrier_semaphore()
    for peer in peers:
        pl.semaphore_signal(barrier, inc=1, device_id=peer, device_id_type=MESH)

    def by_x(p):
        return {"tp": z * 4 + p}

    def by_z(p):
        return {"tp": p * 4 + x}

    tstep, wstep = table.shape[0] // 10, DE // 8
    tload = [
        pltpu.make_async_copy(
            table.at[pl.ds(i * tstep, tstep)], tbuf.at[i % 2], tsem.at[i % 2]
        )
        for i in range(10)
    ]
    wload = [
        pltpu.make_async_copy(w.at[pl.ds(i * wstep, wstep)], wbuf.at[i % 2], wsem.at[i % 2])
        for i in range(8)
    ]
    for i in range(2):
        tload[i].start()
    for i in range(2):
        wload[i].start()
    loads = [
        pltpu.make_async_copy(cached, vc, lsem.at[0]),
        pltpu.make_async_copy(w_self, vs, lsem.at[1]),
        pltpu.make_async_copy(w_query, vq, lsem.at[2]),
    ]
    for i in range(10):
        tload[i].wait()
        wide[pl.ds(i * tstep, tstep), :] = tbuf[i % 2].astype(f32)
        if i + 2 < 10:
            tload[i + 2].start()
    for copy in loads:
        copy.start()

    def look(p):
        def some(k, c):
            for u in range(32):
                found[k * 32 + u, :] = wide[wanted[p, k, u], :]
            return c

        lax.fori_loop(0, CAP // 32, some, 0)
        return found[...].astype(bf16)

    sends = []

    def look_and_send(d):
        p = groups[d]
        rows[p] = look(p)
        copy = remote(rows.at[p], got.at[g], ysend.at[d], yrecv.at[d], {"grp": p})
        copy.start()
        sends.append(copy)

    rows[groups[0]] = look(groups[0])
    pl.semaphore_wait(barrier, len(peers))
    copy = remote(rows.at[groups[0]], got.at[g], ysend.at[0], yrecv.at[0], {"grp": groups[0]})
    copy.start()
    sends.append(copy)
    look_and_send(1)
    for i in range(8):
        wload[i].wait()
        flat = wbuf[i % 2].reshape(wstep, 512)
        at = pl.ds(i * wstep, wstep)
        wx[x, at, :] = flat
        wz[z, at, :] = flat
        if i + 2 < 8:
            wload[i + 2].start()
    ring_x = Ring(wx, x, by_x, [xw.at[i] for i in range(4)])
    ring_z = Ring(wz, z, by_z, [zw.at[i] for i in range(4)])
    ring_x.start()
    ring_z.start()
    for d in range(2, 7):
        look_and_send(d)
    got[g] = look(g)

    loads[0].wait()
    positions = lax.broadcasted_iota(jnp.int32, (8, CACHE), 1)
    for b in range(8):
        spread = head_rows(fresh[0, pl.ds(b, 1), :])
        scores = dot_t(spread.astype(bf16), vc[b, 0]) * ROOT
        fresh_score = jnp.sum(spread * fresh[1, pl.ds(b, 1), :], axis=1, keepdims=True) * ROOT
        live = positions < prefix[b]
        top = jnp.maximum(
            jnp.max(jnp.where(live, scores, -jnp.inf), axis=1, keepdims=True), fresh_score
        )
        raised = jnp.where(live, jnp.exp(scores - top), 0.0)
        fresh_raised = jnp.exp(fresh_score - top)
        total = jnp.sum(raised, axis=1, keepdims=True) + fresh_raised
        weights = (raised / total).astype(bf16)
        fresh_weight = (fresh_raised / total).astype(bf16).astype(f32)
        mixed = dot(weights, vc[b, 1]) + fresh_weight * fresh[2, pl.ds(b, 1), :]
        attended[pl.ds(b, 1), :] = head_pick(mixed)
    loads[1].wait()
    own_sum = Spread(
        attended[...].astype(bf16), vs, part, red, full, [rsems.at[i] for i in range(4)]
    )
    own_sum.start()
    late = pltpu.make_async_copy(w_cross, vs, lsem.at[3])
    late.start()
    own_sum.share()
    own_sum.arrive()
    squares = jnp.zeros((8, 512), f32)
    for c in range(LANES):
        at = pl.ds(c * 512, 512)
        summed = full[c]
        delta[:, at] = summed.astype(bf16)
        r = hidden[:, at].astype(f32) + summed
        squares = squares + r * r
    scale = lax.rsqrt(jnp.sum(squares, axis=1, keepdims=True) / (LANES * 512) + epsilon)
    loads[2].wait()
    asked = jnp.zeros((8, 2 * HD), f32)
    for c in range(LANES):
        at = pl.ds(c * 512, 512)
        r = hidden[:, at].astype(f32) + full[c]
        normed = (r * scale * gain[:, at]).astype(bf16)
        asked = asked + dot(normed, vq[at, :])
    qall[g] = asked.astype(bf16).astype(f32)
    asks = []
    for d, p in enumerate(groups):
        copy = remote(qall.at[g], qall.at[g], qgsend.at[d], qgrecv.at[d], {"grp": p})
        copy.start()
        asks.append(copy)

    ring_x.service()
    ring_z.service()
    for copy in asks:
        copy.wait_recv()
    numbers = lax.broadcasted_iota(jnp.int32, (8, 64), 0) + g * 8
    chosen = (numbers == beams[...]).astype(bf16)
    routed = dot(chosen, qall[...].reshape(64, 2 * HD).astype(bf16))
    qsend_buf[...] = routed
    qx[x] = routed
    qz[z] = routed
    for d in range(1, 4):
        for k, (to, peer, here) in enumerate(((qx, by_x, x), (qz, by_z, z))):
            copy = remote(
                qsend_buf, to.at[here], qtsend.at[k, d - 1], qtrecv.at[k, d - 1],
                peer(lax.rem(here + d, 4)),
            )
            copy.start()
            asks.append(copy)
    ring_x.service_more()
    ring_z.service_more()

    for copy in sends:
        copy.wait_recv()
    for s in range(GROUPS):
        wide[pl.ds(s * CAP, CAP), :] = got[s].astype(f32)

    def put(h, first):
        def beam(b, c):
            def some(k, c):
                line = (first + b) * 4 + h * 2 + k // 4
                column = lax.rem(k, 4) * 32
                for u in range(32):
                    found[k * 32 + u, :] = wide[place[line, column + u], :]
                return c

            lax.fori_loop(0, 8, some, 0)
            placed[h, first + b] = found[0:256, :].astype(bf16)
            return c

        lax.fori_loop(0, 4, beam, 0)

    move_x = Move(placed, 0, xb, x, z, by_x, by_z, xm)
    move_z = Move(placed, 4, zb, z, x, by_z, by_x, zm)
    for h in range(2):
        put(h, 0)
        move_x.exchange(h)
        put(h, 4)
        move_z.exchange(h)
    ring_x.service_last()
    ring_z.service_last()
    for h in range(2):
        move_x.gather(h)
        move_z.gather(h)
    for h in range(2):
        move_x.relay(h)
        move_z.relay(h)
    ring_x.finish()
    ring_z.finish()

    def encode(h, buf, shards, side, turned):
        def piece(p):
            return buf[p % 4, h, p // 4] if turned else buf[p // 4, h, p % 4]

        squares = jnp.zeros((256, HD), f32)
        for p in range(LANES):
            value = piece(p).astype(f32)
            squares = squares + value * value
        scale = lax.rsqrt(jnp.sum(squares, axis=1, keepdims=True) / DE + epsilon)
        for p in range(LANES):
            at = pl.ds(p * HD, HD)
            enc[:, at] = (piece(p).astype(f32) * scale * egain[:, at]).astype(bf16)

        def project(k, carry):
            pairs[side, h, k] = dot(enc[...], shards[k]).astype(bf16)
            return carry

        lax.fori_loop(0, 4, project, 0)

    tokens = lax.broadcasted_iota(jnp.int32, (8, KMAX * NLEN), 1)

    def attend(side, beam, asked):
        live = tokens < counts[g * 8 + beam] * NLEN
        for k in range(4):
            spread = head_rows(asked[k, pl.ds(beam, 1), :]).astype(bf16)
            scores = jnp.concatenate(
                [dot_t(spread, pairs[side, h, k, :, : 2 * HD]) for h in range(2)], axis=1
            )
            scores = jnp.where(live, scores * ROOT, -jnp.inf)
            raised = jnp.exp(scores - jnp.max(scores, axis=1, keepdims=True))
            weights = (raised / jnp.sum(raised, axis=1, keepdims=True)).astype(bf16)
            mixed = dot(weights[:, :256], pairs[side, 0, k, :, 2 * HD :])
            mixed = mixed + dot(weights[:, 256:], pairs[side, 1, k, :, 2 * HD :])
            answer = head_pick(mixed).astype(bf16).astype(f32)
            answers[side, k] = jnp.broadcast_to(answer, (8, 2 * HD))

    for h in range(2):
        move_x.arrive(h)
        encode(h, xb, wx, 0, False)
        move_z.arrive(h)
        encode(h, zb, wz, 1, True)
    for copy in asks[7:]:
        copy.wait_recv()
    attend(0, x, qx)
    replies = []
    for side, beam, here, peer in ((0, x, x, by_x), (1, 4 + z, z, by_z)):
        if side == 1:
            attend(1, 4 + z, qz)
        for d in range(1, 4):
            p = lax.rem(here + d, 4)
            copy = remote(
                answers.at[side, p], ab.at[side, here],
                atsend.at[side, d - 1], atrecv.at[side, d - 1], peer(p),
            )
            copy.start()
            replies.append(copy)
        ab[side, here] = answers[side, here]
    for copy in replies:
        copy.wait_recv()
    aall[g] = jnp.concatenate(
        [ab[0, k, 0:1] for k in range(4)] + [ab[1, k, 0:1] for k in range(4)], axis=0
    )
    returns = []
    for d, p in enumerate(groups):
        copy = remote(aall.at[g], aall.at[g], agsend.at[d], agrecv.at[d], {"grp": p})
        copy.start()
        returns.append(copy)
    late.wait()
    for copy in returns:
        copy.wait_recv()
    picks = (lax.broadcasted_iota(jnp.int32, (8, 64), 1) == slots[...]).astype(bf16)
    held = dot(picks, aall[...].reshape(64, 2 * HD).astype(bf16)).astype(bf16)
    cross_sum = Spread(held, vs, cpart, cred, cfull, [csems.at[i] for i in range(4)])
    cross_sum.start()
    cross_sum.share()
    cross_sum.arrive()
    for c in range(LANES):
        out[:, pl.ds(c * 512, 512)] = cfull[c].astype(bf16)
    own_sum.finish()
    cross_sum.finish()
    move_x.finish()
    move_z.finish()
    for copy in sends + asks + replies + returns:
        copy.wait_send()


def step(wanted, place, prefix, counts, fresh, beams, slots, hidden, gain, egain, *large):
    table, cached, w_self, w_query, w, w_cross = large
    chunk = pltpu.VMEM((LANES, 8, 512), f32)
    shape = jax.ShapeDtypeStruct(hidden.shape, bf16)
    return pl.pallas_call(
        step_kernel,
        out_shape=(shape, shape),
        in_specs=[SMEM] * 4 + [VMEM] * 6 + [ANY] * 6,
        out_specs=(VMEM, VMEM),
        scratch_shapes=[
            pltpu.VMEM((2, table.shape[0] // 10, HD), bf16),
            pltpu.VMEM(table.shape, f32),
            pltpu.VMEM((CAP, HD), f32),
            pltpu.VMEM((GROUPS, CAP, HD), bf16),
            pltpu.VMEM((GROUPS, CAP, HD), bf16),
            pltpu.VMEM((2, DE // 8, 2, 2 * HD), bf16),
            pltpu.VMEM((4, DE, 4 * HD), bf16),
            pltpu.VMEM((4, DE, 4 * HD), bf16),
            pltpu.VMEM(cached.shape, bf16),
            pltpu.VMEM(w_self.shape, bf16),
            pltpu.VMEM(w_query.shape, bf16),
            pltpu.VMEM((8, 2 * HD), f32),
        ]
        + [chunk] * 6
        + [
            pltpu.VMEM((2, 8, 256, HD), bf16),
            pltpu.VMEM((4, 2, 4, 256, HD), bf16),
            pltpu.VMEM((4, 2, 4, 256, HD), bf16),
            pltpu.VMEM((256, DE), bf16),
            pltpu.VMEM((2, 2, 4, 256, 4 * HD), bf16),
            pltpu.VMEM((GROUPS, 8, 2 * HD), f32),
            pltpu.VMEM((8, 2 * HD), f32),
            pltpu.VMEM((4, 8, 2 * HD), f32),
            pltpu.VMEM((4, 8, 2 * HD), f32),
            pltpu.VMEM((2, 4, 8, 2 * HD), f32),
            pltpu.VMEM((2, 4, 8, 2 * HD), f32),
            pltpu.VMEM((GROUPS, 8, 2 * HD), f32),
            DMA((2,)),
            DMA((2,)),
            DMA((4,)),
            DMA((7,)),
            DMA((7,)),
            DMA((4, 15)),
            DMA((4, 15)),
            DMA((4, 3)),
            DMA((4, 3)),
            [DMA((2, 3)), DMA((2, 3)), DMA((2, 3)), DMA((2, 3)), DMA((2,))],
            [DMA((2, 3)), DMA((2, 3)), DMA((2, 3)), DMA((2, 3)), DMA((2,))],
            DMA((7,)),
            DMA((7,)),
            DMA((2, 3)),
            DMA((2, 3)),
            DMA((2, 3)),
            DMA((2, 3)),
            DMA((7,)),
            DMA((7,)),
        ],
        compiler_params=params(0),
        name="step",
    )(wanted, place, prefix, counts, fresh, beams, slots, hidden, gain, egain, *large)


def local(
    neighbour_ids,
    neighbour_shard,
    neighbour_count,
    slot_beam,
    prefix_length,
    embed_table,
    encoder_gain,
    hidden_in,
    decoder_gain,
    fresh_projections,
    cached_pairs,
    w_self_out,
    w_query,
    w_pairs,
    w_cross_out,
):
    me = lax.axis_index("grp")
    shards = neighbour_shard.reshape(neighbour_ids.shape)
    wanted, place = prepare(neighbour_ids, shards, neighbour_count[:, None])
    fresh = jnp.transpose(fresh_projections.astype(f32), (1, 0, 2))
    slots = lax.dynamic_slice_in_dim(slot_beam, me * 8, 8)
    return step(
        wanted, place, prefix_length, neighbour_count, fresh, slot_beam[None, :], slots[:, None],
        hidden_in, decoder_gain[None, :], encoder_gain[None, :],
        embed_table, cached_pairs, w_self_out, w_query, w_pairs, w_cross_out,
    )


def solution(mesh):
    placed = (
        P(),
        P(),
        P(),
        P(),
        P("grp"),
        P("grp", "tp"),
        P(),
        P("grp", None),
        P(),
        P("grp", None, "tp"),
        P("grp", None, None, "tp"),
        P("tp", None),
        P(None, "tp"),
        P(None, None, "tp"),
        P("tp", None),
    )
    return jax.shard_map(
        local,
        mesh=mesh,
        in_specs=placed,
        out_specs=(P("grp", None), P("grp", None)),
        check_vma=False,
    )
```

```python
import math

import jax
import jax.numpy as jnp
from jax import lax
from jax.experimental import pallas as pl
from jax.experimental.pallas import tpu as pltpu
from jax.sharding import PartitionSpec as P

MESH = pl.DeviceIdType.MESH
DMA = pltpu.SemaphoreType.DMA
VMEM = pl.BlockSpec(memory_space=pltpu.VMEM)
SMEM = pl.BlockSpec(memory_space=pltpu.SMEM)
ANY = pl.BlockSpec(memory_space=pl.ANY)

HD = 128
DE = 2048
NLEN = 128
KMAX = 4
CACHE = 512
CAP = 1024
GROUPS = 8
LANES = 16
ROOT = 1.0 / math.sqrt(HD)
epsilon = 1e-05
f32 = jnp.float32
bf16 = jnp.bfloat16
BIG = 62 * 2**20


def params(cid=None):
    if cid is None:
        return pltpu.CompilerParams(vmem_limit_bytes=BIG)
    return pltpu.CompilerParams(collective_id=cid, has_side_effects=True, vmem_limit_bytes=BIG)


def remote(src, dst, send, recv, where):
    return pltpu.make_async_remote_copy(
        src_ref=src, dst_ref=dst, send_sem=send, recv_sem=recv, device_id=where, device_id_type=MESH
    )


def head_rows(row):
    rows = lax.broadcasted_iota(jnp.int32, (8, 2 * HD), 0)
    lanes = lax.broadcasted_iota(jnp.int32, (8, 2 * HD), 1)
    return jnp.where(lanes // HD == rows, jnp.broadcast_to(row, (8, 2 * HD)), 0.0)


def head_pick(full):
    rows = lax.broadcasted_iota(jnp.int32, (8, 2 * HD), 0)
    lanes = lax.broadcasted_iota(jnp.int32, (8, 2 * HD), 1)
    return jnp.sum(jnp.where(lanes // HD == rows, full, 0.0), axis=0, keepdims=True)


def dot(a, b):
    return jnp.dot(a, b, preferred_element_type=f32)


def dot_t(a, b):
    return lax.dot_general(a, b, (((1,), (1,)), ((), ())), preferred_element_type=f32)


def prep_kernel(ids, shards, counts, wanted, place):
    me = lax.axis_index("grp")
    rows = lax.broadcasted_iota(jnp.int32, (256, 1), 0)
    beams = lax.broadcasted_iota(jnp.int32, (256, 64), 1)
    of_beam = lax.broadcasted_iota(jnp.int32, (256, 64), 0) // KMAX == beams
    held = jnp.sum(jnp.where(of_beam, counts[...], 0), axis=1, keepdims=True)
    alive = rows % KMAX < held
    upper = (
        lax.broadcasted_iota(jnp.int32, (NLEN, NLEN), 0)
        <= lax.broadcasted_iota(jnp.int32, (NLEN, NLEN), 1)
    ).astype(bf16)
    down = lax.broadcasted_iota(jnp.int32, (256, 256), 0)
    along = lax.broadcasted_iota(jnp.int32, (256, 256), 1)
    before = ((down // 32 == along // 32) & (along < down)).astype(bf16)
    ones = jnp.ones((NLEN, NLEN), bf16)

    def ranks(mask):
        mask = mask.astype(bf16)
        return dot(mask, upper) + dot(before, dot(mask, ones).astype(bf16)) - 1.0

    mine = (shards[...] == me) & alive
    rank = jnp.where(mine, ranks(mine), -1.0).astype(jnp.int32)
    high, low = rank >> 5, rank & 31
    high = jnp.where(mine, high, -1)
    id_high, id_low = (ids[...] >> 7).astype(f32), (ids[...] & 127).astype(f32)
    small = lax.broadcasted_iota(jnp.int32, (32, NLEN), 0)
    for g in range(GROUPS):
        left, right = [], []
        for i in range(32 * g, 32 * g + 32):
            left.append((small == high[i : i + 1]).astype(bf16))
            spot = small == low[i : i + 1]
            right.append(
                jnp.concatenate(
                    [
                        jnp.where(spot, id_high[i : i + 1], 0.0).astype(bf16),
                        jnp.where(spot, id_low[i : i + 1], 0.0).astype(bf16),
                    ],
                    axis=0,
                )
            )
        both = dot_t(jnp.concatenate(left, axis=1), jnp.concatenate(right, axis=1))
        wanted[g] = (both[:, :32] * 128.0 + both[:, 32:]).astype(jnp.int32)

    at = pl.ds(pl.multiple_of(me * 32, 32), 32)
    own = jnp.concatenate([shards[at, :]] * GROUPS, axis=0)
    beam = me * 8 + lax.broadcasted_iota(jnp.int32, (256, 64), 0) % 32 // KMAX
    own_held = jnp.sum(jnp.where(beam == beams, counts[...], 0), axis=1, keepdims=True)
    named = (own == rows // 32) & (rows % KMAX < own_held)
    spots = jnp.where(named, ranks(named) + (rows // 32 * CAP).astype(f32), 0.0).astype(jnp.int32)
    total = spots[0:32]
    for s in range(1, GROUPS):
        total = total + spots[32 * s : 32 * s + 32]
    place[...] = total


def prepare(ids, shards, counts):
    return pl.pallas_call(
        prep_kernel,
        out_shape=(
            jax.ShapeDtypeStruct((GROUPS, 32, 32), jnp.int32),
            jax.ShapeDtypeStruct((32, NLEN), jnp.int32),
        ),
        in_specs=[VMEM, VMEM, VMEM],
        out_specs=(VMEM, VMEM),
        compiler_params=params(),
        name="prep",
    )(ids, shards, counts)


class Ring:
    def __init__(self, out, here, peer, send, recv):
        up, down, far = lax.rem(here + 1, 4), lax.rem(here + 3, 4), lax.rem(here + 2, 4)
        low, high = pl.ds(0, DE // 2), pl.ds(DE // 2, DE // 2)

        def copy(k, shard, part, to):
            piece = out.at[shard, part]
            return remote(piece, piece, send.at[k], recv.at[k], peer(to))

        self.first = [copy(0, here, low, up), copy(1, here, high, down)]
        self.relays = [copy(2, down, low, up), copy(3, up, high, down)]
        self.second = [copy(4, here, high, up), copy(5, here, low, down)]

    def start(self):
        for copy in self.first:
            copy.start()

    def service(self):
        for copy, relay in zip(self.first, self.relays):
            copy.wait_recv()
            relay.start()
        for copy in self.second:
            copy.start()

    def finish(self):
        for copy in self.relays + self.second:
            copy.wait_recv()
        for copy in self.first + self.relays + self.second:
            copy.wait_send()


class Spread:
    def __init__(self, held, weights, part, red, full, sems):
        self.held, self.weights, self.part, self.red, self.full = held, weights, part, red, full
        self.psend, self.precv, self.asend, self.arecv = sems
        self.t = lax.axis_index("tp")

    def start(self):
        self.reduce = []
        for d in range(1, LANES + 1):
            p = lax.rem(self.t + d, LANES)
            at = pl.ds(pl.multiple_of(p * 512, 512), 512)
            self.part[p] = dot(self.held, self.weights[:, at])
            if d < LANES:
                copy = remote(
                    self.part.at[p], self.red.at[self.t],
                    self.psend.at[d - 1], self.precv.at[d - 1], {"tp": p},
                )
                copy.start()
                self.reduce.append(copy)

    def share(self):
        total = self.part[self.t]
        for d, copy in enumerate(self.reduce):
            copy.wait_recv()
            total = total + self.red[lax.rem(self.t + LANES - 1 - d, LANES)]
        self.full[self.t] = total
        self.shared = []
        for d in range(1, LANES):
            mine = self.full.at[self.t]
            copy = remote(
                mine, mine, self.asend.at[d - 1], self.arecv.at[d - 1],
                {"tp": lax.rem(self.t + d, LANES)},
            )
            copy.start()
            self.shared.append(copy)

    def arrive(self):
        for copy in self.shared:
            copy.wait_recv()

    def finish(self):
        for copy in self.reduce + self.shared:
            copy.wait_send()


class Move:
    def __init__(self, placed, out, core, a, b, peer_a, peer_b, sibling, sems):
        self.asend, self.arecv, self.bsend, self.brecv, self.own = sems
        self.placed, self.out, self.core, self.sibling = placed, out, core, sibling
        self.a, self.b, self.peer_a, self.peer_b = a, b, peer_a, peer_b
        self.exchanged, self.ups, self.downs, self.relays, self.kept = {}, {}, {}, {}, {}

    def exchange_own(self, h):
        a, b, first = self.a, self.b, self.core * 4
        line = []
        for d in (1, 3, 2):
            p = lax.rem(a + d, 4)
            copy = remote(
                self.placed.at[h, first + p], self.out.at[b, h, a, self.core],
                self.asend.at[h, d], self.arecv.at[h, d], self.peer_a(p),
            )
            copy.start()
            line.append(copy)
        self.exchanged[h] = self.exchanged.get(h, []) + line
        self.kept[h] = pltpu.make_async_copy(
            self.placed.at[h, first + a], self.out.at[b, h, a, self.core], self.own.at[h]
        )
        self.kept[h].start()

    def exchange_other(self, h):
        a, b, first = self.a, self.b, (1 - self.core) * 4
        line = []
        for d in (1, 3, 2, 0):
            p = lax.rem(b + d, 4)
            copy = remote(
                self.placed.at[h, first + p], self.out.at[a, h, b, self.core],
                self.asend.at[h, 4 + d], self.arecv.at[h, 4 + d],
                {"grp": self.sibling, **self.peer_b(p)},
            )
            copy.start()
            line.append(copy)
        self.exchanged[h] = self.exchanged.get(h, []) + line

    def gather(self, h):
        self.kept[h].wait()
        for copy in self.exchanged[h]:
            copy.wait_recv()
        mine = self.out.at[self.b, h]
        up, down = lax.rem(self.b + 1, 4), lax.rem(self.b + 3, 4)
        self.ups[h] = remote(
            mine, mine, self.bsend.at[h, 0], self.brecv.at[h, 0], self.peer_b(up)
        )
        self.downs[h] = remote(
            mine, mine, self.bsend.at[h, 1], self.brecv.at[h, 1], self.peer_b(down)
        )
        self.ups[h].start()
        self.downs[h].start()

    def relay(self, h):
        up, down = lax.rem(self.b + 1, 4), lax.rem(self.b + 3, 4)
        if h % 2 == 0:
            self.ups[h].wait_recv()
            piece, to = self.out.at[down, h], up
        else:
            self.downs[h].wait_recv()
            piece, to = self.out.at[up, h], down
        self.relays[h] = remote(
            piece, piece, self.bsend.at[h, 2], self.brecv.at[h, 2], self.peer_b(to)
        )
        self.relays[h].start()

    def arrive(self, h):
        (self.downs if h % 2 == 0 else self.ups)[h].wait_recv()
        self.relays[h].wait_recv()

    def finish(self):
        for h in self.ups:
            for copy in self.exchanged[h]:
                copy.wait_send()
            for copy in (self.ups[h], self.downs[h], self.relays[h]):
                copy.wait_send()


def step_kernel(
    wanted_in, place, prefix, counts, slots, fresh, beams, hidden, gain, egain,
    table, cached, w_self, w_query, w, w_cross,
    delta, out,
    wanted, tbuf, wide, found, rows, got, wbuf, wx, vc, vs, vq, attended,
    part, red, full, cpart, cred, cfull,
    placed, mb, enc, pairs, qall, qsent, qa, answers, ab, aall,
    tsem, wsem, lsem, ysend, yrecv, rsems, csems, rings, ringr, msems,
    qgsend, qgrecv, qtsend, qtrecv, atsend, atrecv, agsend, agrecv,
):
    g, t = lax.axis_index("grp"), lax.axis_index("tp")
    z, x = t // 4, lax.rem(t, 4)
    groups = [lax.rem(g + d, GROUPS) for d in range(1, GROUPS)]
    lanes = [lax.rem(t + d, LANES) for d in range(1, LANES)]
    core = lax.rem(g, 2)
    sibling = g + 1 - 2 * core
    a, b = x * (1 - core) + z * core, z * (1 - core) + x * core

    def by_a(p):
        return {"tp": p * (1 + 3 * core) + (1 - core) * z * 4 + core * x}

    def by_b(p):
        return {"tp": p * (4 - 3 * core) + (1 - core) * x + core * z * 4}

    peers = [{"grp": p} for p in groups] + [{"tp": p} for p in lanes]
    for d in range(1, 4):
        peers.append({"grp": sibling, **by_a(lax.rem(a + d, 4))})
        peers.append({"grp": sibling, **by_b(lax.rem(b + d, 4))})
    barrier = pltpu.get_barrier_semaphore()
    for peer in peers:
        pl.semaphore_signal(barrier, inc=1, device_id=peer, device_id_type=MESH)

    tstep, wstep = table.shape[0] // 10, DE // 8
    tload = [
        pltpu.make_async_copy(
            table.at[pl.ds(i * tstep, tstep)], tbuf.at[i % 5], tsem.at[i % 5]
        )
        for i in range(10)
    ]
    wload = [
        pltpu.make_async_copy(w.at[pl.ds(i * wstep, wstep)], wbuf.at[i % 4], wsem.at[i % 4])
        for i in range(8)
    ]
    loads = [
        pltpu.make_async_copy(cached, vc, lsem.at[0]),
        pltpu.make_async_copy(w_self, vs, lsem.at[1]),
        pltpu.make_async_copy(w_query, vq, lsem.at[2]),
    ]
    for copy in loads[:2]:
        copy.start()
    for i in range(4):
        wload[i].start()
    listed = pltpu.make_async_copy(wanted_in, wanted, lsem.at[4])
    listed.start()
    for i in range(5):
        tload[i].start()
    loads[0].wait()
    positions = lax.broadcasted_iota(jnp.int32, (8, CACHE), 1)
    for n in range(8):
        newest = fresh[n].astype(f32)
        spread = head_rows(newest[0:1])
        scores = dot_t(spread.astype(bf16), vc[n, 0]) * ROOT
        fresh_score = jnp.sum(spread * newest[1:2], axis=1, keepdims=True) * ROOT
        live = positions < prefix[n]
        top = jnp.maximum(
            jnp.max(jnp.where(live, scores, -jnp.inf), axis=1, keepdims=True), fresh_score
        )
        raised = jnp.where(live, jnp.exp(scores - top), 0.0)
        fresh_raised = jnp.exp(fresh_score - top)
        total = jnp.sum(raised, axis=1, keepdims=True) + fresh_raised
        weights = (raised / total).astype(bf16)
        fresh_weight = (fresh_raised / total).astype(bf16).astype(f32)
        mixed = dot(weights, vc[n, 1]) + fresh_weight * newest[2:3]
        attended[pl.ds(n, 1), :] = head_pick(mixed)
    loads[1].wait()
    pl.semaphore_wait(barrier, len(peers))
    own_sum = Spread(
        attended[...].astype(bf16), vs, part, red, full, [rsems.at[i] for i in range(4)]
    )
    own_sum.start()
    for i in range(8):
        wload[i].wait()
        flat = wbuf[i % 4].reshape(wstep, 512)
        at = pl.ds(i * wstep, wstep)
        wx[a, at, :] = flat
        if i + 4 < 8:
            wload[i + 4].start()
    ring = Ring(wx, a, by_a, rings, ringr)
    ring.start()
    loads[2].start()
    late = pltpu.make_async_copy(w_cross, vs, lsem.at[3])
    late.start()
    for i in range(10):
        tload[i].wait()
        wide[pl.ds(i * tstep, tstep), :] = tbuf[i % 5].astype(f32)
        if i + 5 < 10:
            tload[i + 5].start()

    def look(p):
        def some(k, c):
            for u in range(32):
                found[k * 32 + u, :] = wide[wanted[p * CAP + k * 32 + u], :]
            return c

        lax.fori_loop(0, CAP // 32, some, 0)
        return found[...].astype(bf16)

    sends = []

    def look_and_send(d):
        p = groups[d]
        rows[p] = look(p)
        copy = remote(rows.at[p], got.at[g], ysend.at[d], yrecv.at[d], {"grp": p})
        copy.start()
        sends.append(copy)

    listed.wait()
    for d in range(7):
        look_and_send(d)
        if d == 2:
            own_sum.share()
    ring.service()
    got[g] = look(g)
    own_sum.arrive()
    squares = jnp.zeros((8, 512), f32)
    for c in range(LANES):
        at = pl.ds(c * 512, 512)
        summed = full[c]
        delta[:, at] = summed.astype(bf16)
        r = hidden[:, at].astype(f32) + summed
        squares = squares + r * r
    scale = lax.rsqrt(jnp.sum(squares, axis=1, keepdims=True) / (LANES * 512) + epsilon)
    loads[2].wait()
    asked = jnp.zeros((8, 2 * HD), f32)
    for c in range(LANES):
        at = pl.ds(c * 512, 512)
        r = hidden[:, at].astype(f32) + full[c]
        normed = (r * scale * gain[:, at]).astype(bf16)
        asked = asked + dot(normed, vq[at, :])
    qall[g] = asked.astype(bf16).astype(f32)
    asks = []
    for d, p in enumerate(groups):
        copy = remote(qall.at[g], qall.at[g], qgsend.at[d], qgrecv.at[d], {"grp": p})
        copy.start()
        asks.append(copy)


    for copy in sends:
        copy.wait_recv()
    for s in range(GROUPS):
        wide[pl.ds(s * CAP, CAP), :] = got[s].astype(f32)

    def put(h, first):
        def beam(b, c):
            def some(k, c):
                line = (first + b) * 4 + h * 2 + k // 4
                column = lax.rem(k, 4) * 32
                for u in range(32):
                    found[k * 32 + u, :] = wide[place[line, column + u], :]
                return c

            lax.fori_loop(0, 8, some, 0)
            placed[h, first + b] = found[0:256, :].astype(bf16)
            return c

        lax.fori_loop(0, 4, beam, 0)

    move = Move(placed, mb, core, a, b, by_a, by_b, sibling, msems)
    put(0, 4 - 4 * core)
    move.exchange_other(0)
    put(0, 4 * core)
    move.exchange_own(0)
    put(1, 4 - 4 * core)
    put(1, 4 * core)
    move.gather(0)
    move.exchange_other(1)
    move.exchange_own(1)
    move.relay(0)
    move.gather(1)
    for copy in asks:
        copy.wait_recv()
    numbers = lax.broadcasted_iota(jnp.int32, (16, 64), 0) + (g - core) * 8
    chosen = (numbers == beams[...]).astype(bf16)
    routed = dot(chosen, qall[...].reshape(64, 2 * HD).astype(bf16))
    qsent[...] = routed
    qa[a] = routed
    for d in range(1, 4):
        copy = remote(
            qsent, qa.at[a], qtsend.at[d - 1], qtrecv.at[d - 1], by_a(lax.rem(a + d, 4))
        )
        copy.start()
        asks.append(copy)
    ring.finish()

    def encode(h, side):
        def piece(p):
            i, j = p // 4 * (1 - core) + p % 4 * core, p % 4 * (1 - core) + p // 4 * core
            return mb[i, h, j, side]

        squares = jnp.zeros((256, HD), f32)
        for p in range(LANES):
            value = piece(p).astype(f32)
            squares = squares + value * value
        scale = lax.rsqrt(jnp.sum(squares, axis=1, keepdims=True) / DE + epsilon)
        for p in range(LANES):
            at = pl.ds(p * HD, HD)
            enc[:, at] = (piece(p).astype(f32) * scale * egain[:, at]).astype(bf16)

        def project(k, carry):
            pairs[side, h, k] = dot(enc[...], wx[k]).astype(bf16)
            return carry

        lax.fori_loop(0, 4, project, 0)

    tokens = lax.broadcasted_iota(jnp.int32, (8, KMAX * NLEN), 1)

    def attend(side):
        beam = side * 8 + core * 4 + a
        live = tokens < counts[(g - core) * 8 + beam] * NLEN
        for k in range(4):
            spread = head_rows(qa[k, pl.ds(beam, 1), :]).astype(bf16)
            scores = jnp.concatenate(
                [dot_t(spread, pairs[side, h, k, :, : 2 * HD]) for h in range(2)], axis=1
            )
            scores = jnp.where(live, scores * ROOT, -jnp.inf)
            raised = jnp.exp(scores - jnp.max(scores, axis=1, keepdims=True))
            weights = (raised / jnp.sum(raised, axis=1, keepdims=True)).astype(bf16)
            mixed = dot(weights[:, :256], pairs[side, 0, k, :, 2 * HD :])
            mixed = mixed + dot(weights[:, 256:], pairs[side, 1, k, :, 2 * HD :])
            answer = head_pick(mixed).astype(bf16).astype(f32)
            answers[k, pl.ds(side, 1), :] = answer

    move.arrive(0)
    encode(0, 0)
    move.relay(1)
    encode(0, 1)
    for copy in asks[7:]:
        copy.wait_recv()
    move.arrive(1)
    encode(1, 0)
    attend(0)
    encode(1, 1)
    attend(1)
    replies = []
    for d in range(1, 4):
        p = lax.rem(a + d, 4)
        copy = remote(answers.at[p], ab.at[a], atsend.at[d - 1], atrecv.at[d - 1], by_a(p))
        copy.start()
        replies.append(copy)
    ab[a] = answers[a]
    for copy in replies:
        copy.wait_recv()
    aall[g] = jnp.concatenate([ab[k, 0:2] for k in range(4)], axis=0)
    returns = []
    for d, p in enumerate(groups):
        copy = remote(aall.at[g], aall.at[g], agsend.at[d], agrecv.at[d], {"grp": p})
        copy.start()
        returns.append(copy)
    late.wait()
    for copy in returns:
        copy.wait_recv()
    line = lax.broadcasted_iota(jnp.int32, (8, 64), 0)
    decoded = jnp.zeros((8, 64), jnp.int32)
    for j in range(8):
        beam = slots[g * 8 + j]
        held_at = (beam // 16 * 2 + beam // 4 % 2) * 8 + beam % 4 * 2 + beam // 8 % 2
        decoded = jnp.where(line == j, held_at, decoded)
    picks = (lax.broadcasted_iota(jnp.int32, (8, 64), 1) == decoded).astype(bf16)
    held = dot(picks, aall[...].reshape(64, 2 * HD).astype(bf16)).astype(bf16)
    cross_sum = Spread(held, vs, cpart, cred, cfull, [csems.at[i] for i in range(4)])
    cross_sum.start()
    cross_sum.share()
    cross_sum.arrive()
    for c in range(LANES):
        out[:, pl.ds(c * 512, 512)] = cfull[c].astype(bf16)
    own_sum.finish()
    cross_sum.finish()
    move.finish()
    for copy in sends + asks + replies + returns:
        copy.wait_send()


def step(wanted, place, prefix, counts, slots, fresh, beams, hidden, gain, egain, *large):
    table, cached, w_self, w_query, w, w_cross = large
    chunk = pltpu.VMEM((LANES, 8, 512), f32)
    shape = jax.ShapeDtypeStruct(hidden.shape, bf16)
    return pl.pallas_call(
        step_kernel,
        out_shape=(shape, shape),
        in_specs=[ANY] + [SMEM] * 4 + [VMEM] * 5 + [ANY] * 6,
        out_specs=(VMEM, VMEM),
        scratch_shapes=[
            pltpu.SMEM((GROUPS * CAP,), jnp.int32),
            pltpu.VMEM((5, table.shape[0] // 10, HD), bf16),
            pltpu.VMEM(table.shape, f32),
            pltpu.VMEM((CAP, HD), f32),
            pltpu.VMEM((GROUPS, CAP, HD), bf16),
            pltpu.VMEM((GROUPS, CAP, HD), bf16),
            pltpu.VMEM((4, DE // 8, 2, 2 * HD), bf16),
            pltpu.VMEM((4, DE, 4 * HD), bf16),
            pltpu.VMEM(cached.shape, bf16),
            pltpu.VMEM(w_self.shape, bf16),
            pltpu.VMEM(w_query.shape, bf16),
            pltpu.VMEM((8, 2 * HD), f32),
        ]
        + [chunk] * 6
        + [
            pltpu.VMEM((2, 8, 256, HD), bf16),
            pltpu.VMEM((4, 2, 4, 2, 256, HD), bf16),
            pltpu.VMEM((256, DE), bf16),
            pltpu.VMEM((2, 2, 4, 256, 4 * HD), bf16),
            pltpu.VMEM((GROUPS, 8, 2 * HD), f32),
            pltpu.VMEM((16, 2 * HD), f32),
            pltpu.VMEM((4, 16, 2 * HD), f32),
            pltpu.VMEM((4, 8, 2 * HD), f32),
            pltpu.VMEM((4, 8, 2 * HD), f32),
            pltpu.VMEM((GROUPS, 8, 2 * HD), f32),
            DMA((5,)),
            DMA((4,)),
            DMA((5,)),
            DMA((7,)),
            DMA((7,)),
            DMA((4, 15)),
            DMA((4, 15)),
            DMA((6,)),
            DMA((6,)),
            [DMA((2, 8)), DMA((2, 8)), DMA((2, 3)), DMA((2, 3)), DMA((2,))],
            DMA((7,)),
            DMA((7,)),
            DMA((3,)),
            DMA((3,)),
            DMA((3,)),
            DMA((3,)),
            DMA((7,)),
            DMA((7,)),
        ],
        compiler_params=params(0),
        name="step",
    )(wanted, place, prefix, counts, slots, fresh, beams, hidden, gain, egain, *large)


def hand_kernel(delta, out, delta_out, out_out):
    delta_out[...] = delta[...]
    out_out[...] = out[...]


def hand_over(delta, out):
    return pl.pallas_call(
        hand_kernel,
        out_shape=(jax.ShapeDtypeStruct(delta.shape, bf16),) * 2,
        in_specs=[VMEM, VMEM],
        out_specs=(VMEM, VMEM),
        name="hand_over",
    )(delta, out)


def local(
    neighbour_ids,
    neighbour_shard,
    neighbour_count,
    slot_beam,
    prefix_length,
    embed_table,
    encoder_gain,
    hidden_in,
    decoder_gain,
    fresh_projections,
    cached_pairs,
    w_self_out,
    w_query,
    w_pairs,
    w_cross_out,
):
    shards = neighbour_shard.reshape(neighbour_ids.shape)
    wanted, place = prepare(neighbour_ids, shards, neighbour_count[None, :])
    wanted = wanted.reshape(GROUPS * CAP)
    delta, out = step(
        wanted, place, prefix_length, neighbour_count, slot_beam, fresh_projections,
        slot_beam[None, :],        hidden_in, decoder_gain[None, :], encoder_gain[None, :],
        embed_table, cached_pairs, w_self_out, w_query, w_pairs, w_cross_out,
    )
    return hand_over(delta, out)


def solution(mesh):
    placed = (
        P(),
        P(),
        P(),
        P(),
        P("grp"),
        P("grp", "tp"),
        P(),
        P("grp", None),
        P(),
        P("grp", None, "tp"),
        P("grp", None, None, "tp"),
        P("tp", None),
        P(None, "tp"),
        P(None, None, "tp"),
        P("tp", None),
    )
    return jax.shard_map(
        local,
        mesh=mesh,
        in_specs=placed,
        out_specs=(P("grp", None), P("grp", None)),
        check_vma=False,
    )
```

```python
import math

import jax
import jax.numpy as jnp
from jax import lax
from jax.experimental import pallas as pl
from jax.experimental.pallas import tpu as pltpu
from jax.sharding import PartitionSpec as P

MESH = pl.DeviceIdType.MESH
DMA = pltpu.SemaphoreType.DMA
VMEM = pl.BlockSpec(memory_space=pltpu.VMEM)
SMEM = pl.BlockSpec(memory_space=pltpu.SMEM)
ANY = pl.BlockSpec(memory_space=pl.ANY)

HD = 128
DE = 2048
NLEN = 128
KMAX = 4
CACHE = 512
CAP = 1024
GROUPS = 8
LANES = 16
ROOT = 1.0 / math.sqrt(HD)
epsilon = 1e-05
f32 = jnp.float32
bf16 = jnp.bfloat16
BIG = 62 * 2**20


def params(cid=None):
    if cid is None:
        return pltpu.CompilerParams(vmem_limit_bytes=BIG)
    return pltpu.CompilerParams(collective_id=cid, has_side_effects=True, vmem_limit_bytes=BIG)


def remote(src, dst, send, recv, where):
    return pltpu.make_async_remote_copy(
        src_ref=src, dst_ref=dst, send_sem=send, recv_sem=recv, device_id=where, device_id_type=MESH
    )


def head_rows(row):
    rows = lax.broadcasted_iota(jnp.int32, (8, 2 * HD), 0)
    lanes = lax.broadcasted_iota(jnp.int32, (8, 2 * HD), 1)
    return jnp.where(lanes // HD == rows, jnp.broadcast_to(row, (8, 2 * HD)), 0.0)


def head_pick(full):
    rows = lax.broadcasted_iota(jnp.int32, (8, 2 * HD), 0)
    lanes = lax.broadcasted_iota(jnp.int32, (8, 2 * HD), 1)
    return jnp.sum(jnp.where(lanes // HD == rows, full, 0.0), axis=0, keepdims=True)


def dot(a, b):
    return jnp.dot(a, b, preferred_element_type=f32)


def dot_t(a, b):
    return lax.dot_general(a, b, (((1,), (1,)), ((), ())), preferred_element_type=f32)


def prep_kernel(ids, shards, counts, wanted, place):
    me = lax.axis_index("grp")
    rows = lax.broadcasted_iota(jnp.int32, (256, 1), 0)
    beams = lax.broadcasted_iota(jnp.int32, (256, 64), 1)
    of_beam = lax.broadcasted_iota(jnp.int32, (256, 64), 0) // KMAX == beams
    held = jnp.sum(jnp.where(of_beam, counts[...], 0), axis=1, keepdims=True)
    alive = rows % KMAX < held
    upper = (
        lax.broadcasted_iota(jnp.int32, (NLEN, NLEN), 0)
        <= lax.broadcasted_iota(jnp.int32, (NLEN, NLEN), 1)
    ).astype(bf16)
    down = lax.broadcasted_iota(jnp.int32, (256, 256), 0)
    along = lax.broadcasted_iota(jnp.int32, (256, 256), 1)
    before = ((down // 32 == along // 32) & (along < down)).astype(bf16)
    ones = jnp.ones((NLEN, NLEN), bf16)

    def ranks(mask):
        mask = mask.astype(bf16)
        return dot(mask, upper) + dot(before, dot(mask, ones).astype(bf16)) - 1.0

    mine = (shards[...] == me) & alive
    rank = jnp.where(mine, ranks(mine), -1.0).astype(jnp.int32)
    high, low = rank >> 5, rank & 31
    high = jnp.where(mine, high, -1)
    id_high, id_low = (ids[...] >> 7).astype(f32), (ids[...] & 127).astype(f32)
    small = lax.broadcasted_iota(jnp.int32, (32, NLEN), 0)
    for g in range(GROUPS):
        left, right = [], []
        for i in range(32 * g, 32 * g + 32):
            left.append((small == high[i : i + 1]).astype(bf16))
            spot = small == low[i : i + 1]
            right.append(
                jnp.concatenate(
                    [
                        jnp.where(spot, id_high[i : i + 1], 0.0).astype(bf16),
                        jnp.where(spot, id_low[i : i + 1], 0.0).astype(bf16),
                    ],
                    axis=0,
                )
            )
        both = dot_t(jnp.concatenate(left, axis=1), jnp.concatenate(right, axis=1))
        wanted[g] = (both[:, :32] * 128.0 + both[:, 32:]).astype(jnp.int32)

    at = pl.ds(pl.multiple_of(me * 32, 32), 32)
    own = jnp.concatenate([shards[at, :]] * GROUPS, axis=0)
    beam = me * 8 + lax.broadcasted_iota(jnp.int32, (256, 64), 0) % 32 // KMAX
    own_held = jnp.sum(jnp.where(beam == beams, counts[...], 0), axis=1, keepdims=True)
    named = (own == rows // 32) & (rows % KMAX < own_held)
    spots = jnp.where(named, ranks(named) + (rows // 32 * CAP).astype(f32), 0.0).astype(jnp.int32)
    total = spots[0:32]
    for s in range(1, GROUPS):
        total = total + spots[32 * s : 32 * s + 32]
    place[...] = total


def prepare(ids, shards, counts):
    return pl.pallas_call(
        prep_kernel,
        out_shape=(
            jax.ShapeDtypeStruct((GROUPS, 32, 32), jnp.int32),
            jax.ShapeDtypeStruct((32, NLEN), jnp.int32),
        ),
        in_specs=[VMEM, VMEM, VMEM],
        out_specs=(VMEM, VMEM),
        compiler_params=params(),
        name="prep",
    )(ids, shards, counts)


class Ring:
    def __init__(self, out, here, peer, send, recv):
        up, down, far = lax.rem(here + 1, 4), lax.rem(here + 3, 4), lax.rem(here + 2, 4)
        low, high = pl.ds(0, DE // 2), pl.ds(DE // 2, DE // 2)

        def copy(k, shard, part, to):
            piece = out.at[shard, part]
            return remote(piece, piece, send.at[k], recv.at[k], peer(to))

        self.first = [copy(0, here, low, up), copy(1, here, high, down)]
        self.relays = [copy(2, down, low, up), copy(3, up, high, down)]
        self.second = [copy(4, here, high, up), copy(5, here, low, down)]

    def start(self):
        for copy in self.first + self.second:
            copy.start()

    def service(self):
        for copy, relay in zip(self.first, self.relays):
            copy.wait_recv()
            relay.start()

    def finish(self):
        for copy in self.relays + self.second:
            copy.wait_recv()
        for copy in self.first + self.relays + self.second:
            copy.wait_send()


class Spread:
    def __init__(self, held, weights, part, red, full, sems):
        self.held, self.weights, self.part, self.red, self.full = held, weights, part, red, full
        self.psend, self.precv, self.asend, self.arecv = sems
        self.t = lax.axis_index("tp")

    def start(self):
        self.reduce = []
        for d in range(1, LANES + 1):
            p = lax.rem(self.t + d, LANES)
            at = pl.ds(pl.multiple_of(p * 512, 512), 512)
            self.part[p] = dot(self.held, self.weights[:, at])
            if d < LANES:
                copy = remote(
                    self.part.at[p], self.red.at[self.t],
                    self.psend.at[d - 1], self.precv.at[d - 1], {"tp": p},
                )
                copy.start()
                self.reduce.append(copy)

    def share(self):
        total = self.part[self.t]
        for d, copy in enumerate(self.reduce):
            copy.wait_recv()
            total = total + self.red[lax.rem(self.t + LANES - 1 - d, LANES)]
        if self.full.dtype == bf16:
            total = jnp.concatenate([total[:, :256], total[:, 256:]], axis=0).astype(bf16)
        self.full[self.t] = total
        self.shared = []
        for d in range(1, LANES):
            mine = self.full.at[self.t]
            copy = remote(
                mine, mine, self.asend.at[d - 1], self.arecv.at[d - 1],
                {"tp": lax.rem(self.t + d, LANES)},
            )
            copy.start()
            self.shared.append(copy)

    def arrive(self):
        for copy in self.shared:
            copy.wait_recv()

    def finish(self):
        for copy in self.reduce + self.shared:
            copy.wait_send()


class Move:
    def __init__(self, placed, out, core, a, b, peer_a, peer_b, sibling, sems):
        self.asend, self.arecv, self.bsend, self.brecv, self.own = sems
        self.placed, self.out, self.core, self.sibling = placed, out, core, sibling
        self.a, self.b, self.peer_a, self.peer_b = a, b, peer_a, peer_b
        self.exchanged, self.ups, self.downs, self.relays, self.kept = {}, {}, {}, {}, {}

    def exchange_own(self, h):
        a, b, first = self.a, self.b, self.core * 4
        line = []
        for d in (1, 3, 2):
            p = lax.rem(a + d, 4)
            copy = remote(
                self.placed.at[h, first + p], self.out.at[b, h, a, self.core],
                self.asend.at[h, d], self.arecv.at[h, d], self.peer_a(p),
            )
            copy.start()
            line.append(copy)
        self.exchanged[h] = self.exchanged.get(h, []) + line
        self.kept[h] = pltpu.make_async_copy(
            self.placed.at[h, first + a], self.out.at[b, h, a, self.core], self.own.at[h]
        )
        self.kept[h].start()

    def exchange_other(self, h):
        a, b, first = self.a, self.b, (1 - self.core) * 4
        line = []
        for d in (1, 3, 2, 0):
            p = lax.rem(b + d, 4)
            copy = remote(
                self.placed.at[h, first + p], self.out.at[a, h, b, self.core],
                self.asend.at[h, 4 + d], self.arecv.at[h, 4 + d],
                {"grp": self.sibling, **self.peer_b(p)},
            )
            copy.start()
            line.append(copy)
        self.exchanged[h] = self.exchanged.get(h, []) + line

    def gather(self, h):
        self.kept[h].wait()
        for copy in self.exchanged[h]:
            copy.wait_recv()
        mine = self.out.at[self.b, h]
        up, down = lax.rem(self.b + 1, 4), lax.rem(self.b + 3, 4)
        self.ups[h] = remote(
            mine, mine, self.bsend.at[h, 0], self.brecv.at[h, 0], self.peer_b(up)
        )
        self.downs[h] = remote(
            mine, mine, self.bsend.at[h, 1], self.brecv.at[h, 1], self.peer_b(down)
        )
        self.ups[h].start()
        self.downs[h].start()

    def relay(self, h):
        up, down = lax.rem(self.b + 1, 4), lax.rem(self.b + 3, 4)
        if h % 2 == 0:
            self.ups[h].wait_recv()
            piece, to = self.out.at[down, h], up
        else:
            self.downs[h].wait_recv()
            piece, to = self.out.at[up, h], down
        self.relays[h] = remote(
            piece, piece, self.bsend.at[h, 2], self.brecv.at[h, 2], self.peer_b(to)
        )
        self.relays[h].start()

    def arrive(self, h):
        (self.downs if h % 2 == 0 else self.ups)[h].wait_recv()
        self.relays[h].wait_recv()

    def finish(self):
        for h in self.ups:
            for copy in self.exchanged[h]:
                copy.wait_send()
            for copy in (self.ups[h], self.downs[h], self.relays[h]):
                copy.wait_send()


def step_kernel(
    wanted_in, place, prefix, counts, slots, fresh, beams, hidden, gain, egain,
    table, cached, w_self, w_query, w, w_cross,
    delta, out,
    wanted, tbuf, wide, found, rows, got, wbuf, wx, vc, vs, vq, attended,
    part, red, full, cpart, cred, cfull,
    placed, mb, enc, pairs, qall, qsent, qa, answers, ab, aall,
    tsem, wsem, lsem, ysend, yrecv, rsems, csems, rings, ringr, msems,
    qgsend, qgrecv, qtsend, qtrecv, atsend, atrecv, agsend, agrecv,
):
    g, t = lax.axis_index("grp"), lax.axis_index("tp")
    z, x = t // 4, lax.rem(t, 4)
    groups = [lax.rem(g + d, GROUPS) for d in range(1, GROUPS)]
    lanes = [lax.rem(t + d, LANES) for d in range(1, LANES)]
    core = lax.rem(g, 2)
    sibling = g + 1 - 2 * core
    a, b = x * (1 - core) + z * core, z * (1 - core) + x * core

    def by_a(p):
        return {"tp": p * (1 + 3 * core) + (1 - core) * z * 4 + core * x}

    def by_b(p):
        return {"tp": p * (4 - 3 * core) + (1 - core) * x + core * z * 4}

    peers = [{"grp": p} for p in groups] + [{"tp": p} for p in lanes]
    for d in range(1, 4):
        peers.append({"grp": sibling, **by_a(lax.rem(a + d, 4))})
        peers.append({"grp": sibling, **by_b(lax.rem(b + d, 4))})
    barrier = pltpu.get_barrier_semaphore()
    for peer in peers:
        pl.semaphore_signal(barrier, inc=1, device_id=peer, device_id_type=MESH)

    tstep, wstep = table.shape[0] // 10, DE // 8
    tload = [
        pltpu.make_async_copy(
            table.at[pl.ds(i * tstep, tstep)], tbuf.at[i % 5], tsem.at[i % 5]
        )
        for i in range(10)
    ]
    wload = [
        pltpu.make_async_copy(w.at[pl.ds(i * wstep, wstep)], wbuf.at[i % 4], wsem.at[i % 4])
        for i in range(8)
    ]
    loads = [
        pltpu.make_async_copy(cached, vc, lsem.at[0]),
        pltpu.make_async_copy(w_self, vs, lsem.at[1]),
        pltpu.make_async_copy(w_query, vq, lsem.at[2]),
    ]
    for copy in loads[:2]:
        copy.start()
    for i in range(4):
        wload[i].start()
    listed = pltpu.make_async_copy(wanted_in, wanted, lsem.at[4])
    listed.start()
    for i in range(5):
        tload[i].start()
    loads[0].wait()
    positions = lax.broadcasted_iota(jnp.int32, (8, CACHE), 1)
    for n in range(8):
        newest = fresh[n].astype(f32)
        spread = head_rows(newest[0:1])
        scores = dot_t(spread.astype(bf16), vc[n, 0]) * ROOT
        fresh_score = jnp.sum(spread * newest[1:2], axis=1, keepdims=True) * ROOT
        live = positions < prefix[n]
        top = jnp.maximum(
            jnp.max(jnp.where(live, scores, -jnp.inf), axis=1, keepdims=True), fresh_score
        )
        raised = jnp.where(live, jnp.exp(scores - top), 0.0)
        fresh_raised = jnp.exp(fresh_score - top)
        total = jnp.sum(raised, axis=1, keepdims=True) + fresh_raised
        weights = (raised / total).astype(bf16)
        fresh_weight = (fresh_raised / total).astype(bf16).astype(f32)
        mixed = dot(weights, vc[n, 1]) + fresh_weight * newest[2:3]
        attended[pl.ds(n, 1), :] = head_pick(mixed)
    loads[1].wait()
    pl.semaphore_wait(barrier, len(peers))
    own_sum = Spread(
        attended[...].astype(bf16), vs, part, red, full, [rsems.at[i] for i in range(4)]
    )
    own_sum.start()
    for i in range(8):
        wload[i].wait()
        flat = wbuf[i % 4].reshape(wstep, 512)
        at = pl.ds(i * wstep, wstep)
        wx[a, at, :] = flat
        if i + 4 < 8:
            wload[i + 4].start()
    ring = Ring(wx, a, by_a, rings, ringr)
    ring.start()
    loads[2].start()
    late = pltpu.make_async_copy(w_cross, vs, lsem.at[3])
    late.start()
    for i in range(10):
        tload[i].wait()
        wide[pl.ds(i * tstep, tstep), :] = tbuf[i % 5].astype(f32)
        if i + 5 < 10:
            tload[i + 5].start()

    def look(p):
        def some(k, c):
            for u in range(32):
                found[k * 32 + u, :] = wide[wanted[p * CAP + k * 32 + u], :]
            return c

        lax.fori_loop(0, CAP // 32, some, 0)
        return found[...].astype(bf16)

    sends = []

    def look_and_send(d):
        p = groups[d]
        rows[p] = look(p)
        copy = remote(rows.at[p], got.at[g], ysend.at[d], yrecv.at[d], {"grp": p})
        copy.start()
        sends.append(copy)

    listed.wait()
    for d in range(7):
        look_and_send(d)
        if d == 2:
            own_sum.share()
    ring.service()
    got[g] = look(g)
    own_sum.arrive()
    squares = jnp.zeros((8, 512), f32)
    for c in range(LANES):
        at = pl.ds(c * 512, 512)
        summed = full[c]
        delta[:, at] = summed.astype(bf16)
        r = hidden[:, at].astype(f32) + summed
        squares = squares + r * r
    scale = lax.rsqrt(jnp.sum(squares, axis=1, keepdims=True) / (LANES * 512) + epsilon)
    loads[2].wait()
    asked = jnp.zeros((8, 2 * HD), f32)
    for c in range(LANES):
        at = pl.ds(c * 512, 512)
        r = hidden[:, at].astype(f32) + full[c]
        normed = (r * scale * gain[:, at]).astype(bf16)
        asked = asked + dot(normed, vq[at, :])
    qall[g] = asked.astype(bf16).astype(f32)
    asks = []
    for d, p in enumerate(groups):
        copy = remote(qall.at[g], qall.at[g], qgsend.at[d], qgrecv.at[d], {"grp": p})
        copy.start()
        asks.append(copy)


    for copy in sends:
        copy.wait_recv()
    for s in range(GROUPS):
        wide[pl.ds(s * CAP, CAP), :] = got[s].astype(f32)

    def put(h, first):
        def beam(b, c):
            def some(k, c):
                line = (first + b) * 4 + h * 2 + k // 4
                column = lax.rem(k, 4) * 32
                for u in range(32):
                    found[k * 32 + u, :] = wide[place[line, column + u], :]
                return c

            lax.fori_loop(0, 8, some, 0)
            placed[h, first + b] = found[0:256, :].astype(bf16)
            return c

        lax.fori_loop(0, 4, beam, 0)

    move = Move(placed, mb, core, a, b, by_a, by_b, sibling, msems)
    put(0, 4 - 4 * core)
    move.exchange_other(0)
    put(0, 4 * core)
    move.exchange_own(0)
    put(1, 4 - 4 * core)
    move.exchange_other(1)
    move.gather(0)
    put(1, 4 * core)
    move.exchange_own(1)
    move.relay(0)
    move.gather(1)
    move.relay(1)
    for copy in asks:
        copy.wait_recv()
    numbers = lax.broadcasted_iota(jnp.int32, (16, 64), 0) + (g - core) * 8
    chosen = (numbers == beams[...]).astype(bf16)
    routed = dot(chosen, qall[...].reshape(64, 2 * HD).astype(bf16))
    qsent[...] = routed
    qa[a] = routed
    for d in range(1, 4):
        copy = remote(
            qsent, qa.at[a], qtsend.at[d - 1], qtrecv.at[d - 1], by_a(lax.rem(a + d, 4))
        )
        copy.start()
        asks.append(copy)
    ring.finish()

    def encode(h, side):
        def piece(p):
            i, j = p // 4 * (1 - core) + p % 4 * core, p % 4 * (1 - core) + p // 4 * core
            return mb[i, h, j, side]

        squares = jnp.zeros((256, HD), f32)
        for p in range(LANES):
            value = piece(p).astype(f32)
            squares = squares + value * value
        scale = lax.rsqrt(jnp.sum(squares, axis=1, keepdims=True) / DE + epsilon)
        for p in range(LANES):
            at = pl.ds(p * HD, HD)
            enc[:, at] = (piece(p).astype(f32) * scale * egain[:, at]).astype(bf16)

        def project(k, carry):
            pairs[side, h, k] = dot(enc[...], wx[k]).astype(bf16)
            return carry

        lax.fori_loop(0, 4, project, 0)

    tokens = lax.broadcasted_iota(jnp.int32, (8, KMAX * NLEN), 1)

    def attend(side):
        beam = side * 8 + core * 4 + a
        live = tokens < counts[(g - core) * 8 + beam] * NLEN
        for k in range(4):
            spread = head_rows(qa[k, pl.ds(beam, 1), :]).astype(bf16)
            scores = jnp.concatenate(
                [dot_t(spread, pairs[side, h, k, :, : 2 * HD]) for h in range(2)], axis=1
            )
            scores = jnp.where(live, scores * ROOT, -jnp.inf)
            raised = jnp.exp(scores - jnp.max(scores, axis=1, keepdims=True))
            weights = (raised / jnp.sum(raised, axis=1, keepdims=True)).astype(bf16)
            mixed = dot(weights[:, :256], pairs[side, 0, k, :, 2 * HD :])
            mixed = mixed + dot(weights[:, 256:], pairs[side, 1, k, :, 2 * HD :])
            answer = head_pick(mixed).astype(bf16).astype(f32)
            answers[k, pl.ds(side, 1), :] = answer

    move.arrive(0)
    encode(0, 0)
    encode(0, 1)
    for copy in asks[7:]:
        copy.wait_recv()
    move.arrive(1)
    encode(1, 0)
    attend(0)
    encode(1, 1)
    attend(1)
    replies = []
    for d in range(1, 4):
        p = lax.rem(a + d, 4)
        copy = remote(answers.at[p], ab.at[a], atsend.at[d - 1], atrecv.at[d - 1], by_a(p))
        copy.start()
        replies.append(copy)
    ab[a] = answers[a]
    for copy in replies:
        copy.wait_recv()
    aall[g] = jnp.concatenate([ab[k, 0:2] for k in range(4)], axis=0)
    returns = []
    for d, p in enumerate(groups):
        copy = remote(aall.at[g], aall.at[g], agsend.at[d], agrecv.at[d], {"grp": p})
        copy.start()
        returns.append(copy)
    late.wait()
    for copy in returns:
        copy.wait_recv()
    line = lax.broadcasted_iota(jnp.int32, (8, 64), 0)
    decoded = jnp.zeros((8, 64), jnp.int32)
    for j in range(8):
        beam = slots[g * 8 + j]
        held_at = (beam // 16 * 2 + beam // 4 % 2) * 8 + beam % 4 * 2 + beam // 8 % 2
        decoded = jnp.where(line == j, held_at, decoded)
    picks = (lax.broadcasted_iota(jnp.int32, (8, 64), 1) == decoded).astype(bf16)
    held = dot(picks, aall[...].reshape(64, 2 * HD).astype(bf16)).astype(bf16)
    cross_sum = Spread(held, vs, cpart, cred, cfull, [csems.at[i] for i in range(4)])
    cross_sum.start()
    cross_sum.share()
    cross_sum.arrive()
    for c in range(LANES):
        both = cfull[c].astype(f32)
        out[:, pl.ds(c * 512, 256)] = both[:8].astype(bf16)
        out[:, pl.ds(c * 512 + 256, 256)] = both[8:].astype(bf16)
    own_sum.finish()
    cross_sum.finish()
    move.finish()
    for copy in sends + asks + replies + returns:
        copy.wait_send()


def step(wanted, place, prefix, counts, slots, fresh, beams, hidden, gain, egain, *large):
    table, cached, w_self, w_query, w, w_cross = large
    chunk = pltpu.VMEM((LANES, 8, 512), f32)
    shape = jax.ShapeDtypeStruct(hidden.shape, bf16)
    return pl.pallas_call(
        step_kernel,
        out_shape=(shape, shape),
        in_specs=[ANY] + [SMEM] * 4 + [VMEM] * 5 + [ANY] * 6,
        out_specs=(VMEM, VMEM),
        scratch_shapes=[
            pltpu.SMEM((GROUPS * CAP,), jnp.int32),
            pltpu.VMEM((5, table.shape[0] // 10, HD), bf16),
            pltpu.VMEM(table.shape, f32),
            pltpu.VMEM((CAP, HD), f32),
            pltpu.VMEM((GROUPS, CAP, HD), bf16),
            pltpu.VMEM((GROUPS, CAP, HD), bf16),
            pltpu.VMEM((4, DE // 8, 2, 2 * HD), bf16),
            pltpu.VMEM((4, DE, 4 * HD), bf16),
            pltpu.VMEM(cached.shape, bf16),
            pltpu.VMEM(w_self.shape, bf16),
            pltpu.VMEM(w_query.shape, bf16),
            pltpu.VMEM((8, 2 * HD), f32),
        ]
        + [chunk] * 5
        + [
            pltpu.VMEM((LANES, 16, 256), bf16),
            pltpu.VMEM((2, 8, 256, HD), bf16),
            pltpu.VMEM((4, 2, 4, 2, 256, HD), bf16),
            pltpu.VMEM((256, DE), bf16),
            pltpu.VMEM((2, 2, 4, 256, 4 * HD), bf16),
            pltpu.VMEM((GROUPS, 8, 2 * HD), f32),
            pltpu.VMEM((16, 2 * HD), f32),
            pltpu.VMEM((4, 16, 2 * HD), f32),
            pltpu.VMEM((4, 8, 2 * HD), f32),
            pltpu.VMEM((4, 8, 2 * HD), f32),
            pltpu.VMEM((GROUPS, 8, 2 * HD), f32),
            DMA((5,)),
            DMA((4,)),
            DMA((5,)),
            DMA((7,)),
            DMA((7,)),
            DMA((4, 15)),
            DMA((4, 15)),
            DMA((6,)),
            DMA((6,)),
            [DMA((2, 8)), DMA((2, 8)), DMA((2, 3)), DMA((2, 3)), DMA((2,))],
            DMA((7,)),
            DMA((7,)),
            DMA((3,)),
            DMA((3,)),
            DMA((3,)),
            DMA((3,)),
            DMA((7,)),
            DMA((7,)),
        ],
        compiler_params=params(0),
        name="step",
    )(wanted, place, prefix, counts, slots, fresh, beams, hidden, gain, egain, *large)


def hand_kernel(delta, out, delta_out, out_out):
    delta_out[...] = delta[...]
    out_out[...] = out[...]


def hand_over(delta, out):
    return pl.pallas_call(
        hand_kernel,
        out_shape=(jax.ShapeDtypeStruct(delta.shape, bf16),) * 2,
        in_specs=[VMEM, VMEM],
        out_specs=(VMEM, VMEM),
        name="hand_over",
    )(delta, out)


def local(
    neighbour_ids,
    neighbour_shard,
    neighbour_count,
    slot_beam,
    prefix_length,
    embed_table,
    encoder_gain,
    hidden_in,
    decoder_gain,
    fresh_projections,
    cached_pairs,
    w_self_out,
    w_query,
    w_pairs,
    w_cross_out,
):
    shards = neighbour_shard.reshape(neighbour_ids.shape)
    wanted, place = prepare(neighbour_ids, shards, neighbour_count[None, :])
    wanted = wanted.reshape(GROUPS * CAP)
    delta, out = step(
        wanted, place, prefix_length, neighbour_count, slot_beam, fresh_projections,
        slot_beam[None, :],        hidden_in, decoder_gain[None, :], encoder_gain[None, :],
        embed_table, cached_pairs, w_self_out, w_query, w_pairs, w_cross_out,
    )
    return hand_over(delta, out)


def solution(mesh):
    placed = (
        P(),
        P(),
        P(),
        P(),
        P("grp"),
        P("grp", "tp"),
        P(),
        P("grp", None),
        P(),
        P("grp", None, "tp"),
        P("grp", None, None, "tp"),
        P("tp", None),
        P(None, "tp"),
        P(None, None, "tp"),
        P("tp", None),
    )
    return jax.shard_map(
        local,
        mesh=mesh,
        in_specs=placed,
        out_specs=(P("grp", None), P("grp", None)),
        check_vma=False,
    )
```

```python
import math

import jax
import jax.numpy as jnp
from jax import lax
from jax.experimental import pallas as pl
from jax.experimental.pallas import tpu as pltpu
from jax.sharding import PartitionSpec as P

MESH = pl.DeviceIdType.MESH
DMA = pltpu.SemaphoreType.DMA
VMEM = pl.BlockSpec(memory_space=pltpu.VMEM)
SMEM = pl.BlockSpec(memory_space=pltpu.SMEM)
ANY = pl.BlockSpec(memory_space=pl.ANY)

HD = 128
DE = 2048
NLEN = 128
KMAX = 4
CACHE = 512
CAP = 1024
GROUPS = 8
LANES = 16
ROOT = 1.0 / math.sqrt(HD)
epsilon = 1e-05
f32 = jnp.float32
bf16 = jnp.bfloat16
BIG = 62 * 2**20


def params(cid=None):
    if cid is None:
        return pltpu.CompilerParams(vmem_limit_bytes=BIG)
    return pltpu.CompilerParams(collective_id=cid, has_side_effects=True, vmem_limit_bytes=BIG)


def remote(src, dst, send, recv, where):
    return pltpu.make_async_remote_copy(
        src_ref=src, dst_ref=dst, send_sem=send, recv_sem=recv, device_id=where, device_id_type=MESH
    )


def head_rows(row):
    rows = lax.broadcasted_iota(jnp.int32, (8, 2 * HD), 0)
    lanes = lax.broadcasted_iota(jnp.int32, (8, 2 * HD), 1)
    return jnp.where(lanes // HD == rows, jnp.broadcast_to(row, (8, 2 * HD)), 0.0)


def head_pick(full):
    rows = lax.broadcasted_iota(jnp.int32, (8, 2 * HD), 0)
    lanes = lax.broadcasted_iota(jnp.int32, (8, 2 * HD), 1)
    return jnp.sum(jnp.where(lanes // HD == rows, full, 0.0), axis=0, keepdims=True)


def dot(a, b):
    return jnp.dot(a, b, preferred_element_type=f32)


def dot_t(a, b):
    return lax.dot_general(a, b, (((1,), (1,)), ((), ())), preferred_element_type=f32)


def prep_kernel(ids, shards, counts, wanted, place):
    me = lax.axis_index("grp")
    rows = lax.broadcasted_iota(jnp.int32, (256, 1), 0)
    beams = lax.broadcasted_iota(jnp.int32, (256, 64), 1)
    of_beam = lax.broadcasted_iota(jnp.int32, (256, 64), 0) // KMAX == beams
    held = jnp.sum(jnp.where(of_beam, counts[...], 0), axis=1, keepdims=True)
    alive = rows % KMAX < held
    upper = (
        lax.broadcasted_iota(jnp.int32, (NLEN, NLEN), 0)
        <= lax.broadcasted_iota(jnp.int32, (NLEN, NLEN), 1)
    ).astype(bf16)
    down = lax.broadcasted_iota(jnp.int32, (256, 256), 0)
    along = lax.broadcasted_iota(jnp.int32, (256, 256), 1)
    before = ((down // 32 == along // 32) & (along < down)).astype(bf16)
    ones = jnp.ones((NLEN, NLEN), bf16)

    def ranks(mask):
        mask = mask.astype(bf16)
        return dot(mask, upper) + dot(before, dot(mask, ones).astype(bf16)) - 1.0

    mine = (shards[...] == me) & alive
    rank = jnp.where(mine, ranks(mine), -1.0).astype(jnp.int32)
    high, low = rank >> 5, rank & 31
    high = jnp.where(mine, high, -1)
    id_high, id_low = (ids[...] >> 7).astype(f32), (ids[...] & 127).astype(f32)
    small = lax.broadcasted_iota(jnp.int32, (32, NLEN), 0)
    for g in range(GROUPS):
        left, right = [], []
        for i in range(32 * g, 32 * g + 32):
            left.append((small == high[i : i + 1]).astype(bf16))
            spot = small == low[i : i + 1]
            right.append(
                jnp.concatenate(
                    [
                        jnp.where(spot, id_high[i : i + 1], 0.0).astype(bf16),
                        jnp.where(spot, id_low[i : i + 1], 0.0).astype(bf16),
                    ],
                    axis=0,
                )
            )
        both = dot_t(jnp.concatenate(left, axis=1), jnp.concatenate(right, axis=1))
        wanted[g] = (both[:, :32] * 128.0 + both[:, 32:]).astype(jnp.int32)

    at = pl.ds(pl.multiple_of(me * 32, 32), 32)
    own = jnp.concatenate([shards[at, :]] * GROUPS, axis=0)
    beam = me * 8 + lax.broadcasted_iota(jnp.int32, (256, 64), 0) % 32 // KMAX
    own_held = jnp.sum(jnp.where(beam == beams, counts[...], 0), axis=1, keepdims=True)
    named = (own == rows // 32) & (rows % KMAX < own_held)
    spots = jnp.where(named, ranks(named) + (rows // 32 * CAP).astype(f32), 0.0).astype(jnp.int32)
    total = spots[0:32]
    for s in range(1, GROUPS):
        total = total + spots[32 * s : 32 * s + 32]
    place[...] = total


def prepare(ids, shards, counts):
    return pl.pallas_call(
        prep_kernel,
        out_shape=(
            jax.ShapeDtypeStruct((GROUPS, 32, 32), jnp.int32),
            jax.ShapeDtypeStruct((32, NLEN), jnp.int32),
        ),
        in_specs=[VMEM, VMEM, VMEM],
        out_specs=(VMEM, VMEM),
        compiler_params=params(),
        name="prep",
    )(ids, shards, counts)


class Ring:
    def __init__(self, out, here, peer, send, recv):
        up, down, far = lax.rem(here + 1, 4), lax.rem(here + 3, 4), lax.rem(here + 2, 4)
        low, high = pl.ds(0, DE // 2), pl.ds(DE // 2, DE // 2)

        def copy(k, shard, part, to):
            piece = out.at[shard, part]
            return remote(piece, piece, send.at[k], recv.at[k], peer(to))

        self.first = [copy(0, here, low, up), copy(1, here, high, down)]
        self.relays = [copy(2, down, low, up), copy(3, up, high, down)]
        self.second = [copy(4, here, high, up), copy(5, here, low, down)]

    def start(self):
        for copy in self.first + self.second:
            copy.start()

    def service(self):
        for copy, relay in zip(self.first, self.relays):
            copy.wait_recv()
            relay.start()

    def finish(self):
        for copy in self.relays + self.second:
            copy.wait_recv()
        for copy in self.first + self.relays + self.second:
            copy.wait_send()


class Spread:
    def __init__(self, held, weights, part, red, full, sems):
        self.held, self.weights, self.part, self.red, self.full = held, weights, part, red, full
        self.psend, self.precv, self.asend, self.arecv = sems
        self.t = lax.axis_index("tp")

    def start(self):
        self.reduce = []
        for d in range(1, LANES + 1):
            p = lax.rem(self.t + d, LANES)
            at = pl.ds(pl.multiple_of(p * 512, 512), 512)
            self.part[p] = dot(self.held, self.weights[:, at])
            if d < LANES:
                copy = remote(
                    self.part.at[p], self.red.at[self.t],
                    self.psend.at[d - 1], self.precv.at[d - 1], {"tp": p},
                )
                copy.start()
                self.reduce.append(copy)

    def share(self):
        total = self.part[self.t]
        for d, copy in enumerate(self.reduce):
            copy.wait_recv()
            total = total + self.red[lax.rem(self.t + LANES - 1 - d, LANES)]
        if self.full.dtype == bf16:
            total = jnp.concatenate([total[:, :256], total[:, 256:]], axis=0).astype(bf16)
        self.full[self.t] = total
        self.shared = []
        for d in range(1, LANES):
            mine = self.full.at[self.t]
            copy = remote(
                mine, mine, self.asend.at[d - 1], self.arecv.at[d - 1],
                {"tp": lax.rem(self.t + d, LANES)},
            )
            copy.start()
            self.shared.append(copy)

    def arrive(self):
        for copy in self.shared:
            copy.wait_recv()

    def finish(self):
        for copy in self.reduce + self.shared:
            copy.wait_send()


class Move:
    def __init__(self, placed, out, core, a, b, peer_a, peer_b, sibling, sems):
        self.asend, self.arecv, self.bsend, self.brecv, self.own = sems
        self.placed, self.out, self.core, self.sibling = placed, out, core, sibling
        self.a, self.b, self.peer_a, self.peer_b = a, b, peer_a, peer_b
        self.exchanged, self.ups, self.downs, self.relays, self.kept = {}, {}, {}, {}, {}

    def exchange_own(self, h):
        a, b, first = self.a, self.b, self.core * 4
        line = []
        for d in (1, 3, 2):
            p = lax.rem(a + d, 4)
            copy = remote(
                self.placed.at[h, first + p], self.out.at[b, h, a, self.core],
                self.asend.at[h, d], self.arecv.at[h, d], self.peer_a(p),
            )
            copy.start()
            line.append(copy)
        self.exchanged[h] = self.exchanged.get(h, []) + line
        self.kept[h] = pltpu.make_async_copy(
            self.placed.at[h, first + a], self.out.at[b, h, a, self.core], self.own.at[h]
        )
        self.kept[h].start()

    def exchange_other(self, h):
        a, b, first = self.a, self.b, (1 - self.core) * 4
        line = []
        for d in (1, 3, 2, 0):
            p = lax.rem(b + d, 4)
            copy = remote(
                self.placed.at[h, first + p], self.out.at[a, h, b, self.core],
                self.asend.at[h, 4 + d], self.arecv.at[h, 4 + d],
                {"grp": self.sibling, **self.peer_b(p)},
            )
            copy.start()
            line.append(copy)
        self.exchanged[h] = self.exchanged.get(h, []) + line

    def gather(self, h):
        self.kept[h].wait()
        for copy in self.exchanged[h]:
            copy.wait_recv()
        mine = self.out.at[self.b, h]
        up, down = lax.rem(self.b + 1, 4), lax.rem(self.b + 3, 4)
        self.ups[h] = remote(
            mine, mine, self.bsend.at[h, 0], self.brecv.at[h, 0], self.peer_b(up)
        )
        self.downs[h] = remote(
            mine, mine, self.bsend.at[h, 1], self.brecv.at[h, 1], self.peer_b(down)
        )
        self.ups[h].start()
        self.downs[h].start()

    def relay(self, h):
        up, down = lax.rem(self.b + 1, 4), lax.rem(self.b + 3, 4)
        if h % 2 == 0:
            self.ups[h].wait_recv()
            piece, to = self.out.at[down, h], up
        else:
            self.downs[h].wait_recv()
            piece, to = self.out.at[up, h], down
        self.relays[h] = remote(
            piece, piece, self.bsend.at[h, 2], self.brecv.at[h, 2], self.peer_b(to)
        )
        self.relays[h].start()

    def arrive(self, h):
        (self.downs if h % 2 == 0 else self.ups)[h].wait_recv()
        self.relays[h].wait_recv()

    def finish(self):
        for h in self.ups:
            for copy in self.exchanged[h]:
                copy.wait_send()
            for copy in (self.ups[h], self.downs[h], self.relays[h]):
                copy.wait_send()


def step_kernel(
    wanted_in, place, prefix, counts, slots, fresh, beams, hidden, gain, egain,
    table, cached, w_self, w_query, w, w_cross,
    delta, out,
    wanted, tbuf, wide, found, rows, got, wbuf, wx, vc, vs, vq, attended,
    part, red, full, cpart, cred, cfull,
    placed, mb, enc, pairs, qall, qsent, qa, answers, ab, aall,
    tsem, wsem, lsem, ysend, yrecv, rsems, csems, rings, ringr, msems,
    qgsend, qgrecv, qtsend, qtrecv, atsend, atrecv, agsend, agrecv,
):
    g, t = lax.axis_index("grp"), lax.axis_index("tp")
    z, x = t // 4, lax.rem(t, 4)
    groups = [lax.rem(g + d, GROUPS) for d in range(1, GROUPS)]
    lanes = [lax.rem(t + d, LANES) for d in range(1, LANES)]
    core = lax.rem(g, 2)
    sibling = g + 1 - 2 * core
    a, b = x * (1 - core) + z * core, z * (1 - core) + x * core

    def by_a(p):
        return {"tp": p * (1 + 3 * core) + (1 - core) * z * 4 + core * x}

    def by_b(p):
        return {"tp": p * (4 - 3 * core) + (1 - core) * x + core * z * 4}

    peers = [{"grp": p} for p in groups] + [{"tp": p} for p in lanes]
    for d in range(1, 4):
        peers.append({"grp": sibling, **by_a(lax.rem(a + d, 4))})
        peers.append({"grp": sibling, **by_b(lax.rem(b + d, 4))})
    barrier = pltpu.get_barrier_semaphore()
    for peer in peers:
        pl.semaphore_signal(barrier, inc=1, device_id=peer, device_id_type=MESH)

    tstep, wstep = table.shape[0] // 10, DE // 8
    tload = [
        pltpu.make_async_copy(
            table.at[pl.ds(i * tstep, tstep)], tbuf.at[i % 5], tsem.at[i % 5]
        )
        for i in range(10)
    ]
    wload = [
        pltpu.make_async_copy(w.at[pl.ds(i * wstep, wstep)], wbuf.at[i % 4], wsem.at[i % 4])
        for i in range(8)
    ]
    loads = [
        pltpu.make_async_copy(cached, vc, lsem.at[0]),
        pltpu.make_async_copy(w_self, vs, lsem.at[1]),
        pltpu.make_async_copy(w_query, vq, lsem.at[2]),
    ]
    for copy in loads[:2]:
        copy.start()
    for i in range(4):
        wload[i].start()
    listed = pltpu.make_async_copy(wanted_in, wanted, lsem.at[4])
    listed.start()
    for i in range(5):
        tload[i].start()
    loads[0].wait()
    positions = lax.broadcasted_iota(jnp.int32, (8, CACHE), 1)
    for n in range(8):
        newest = fresh[n].astype(f32)
        spread = head_rows(newest[0:1])
        scores = dot_t(spread.astype(bf16), vc[n, 0]) * ROOT
        fresh_score = jnp.sum(spread * newest[1:2], axis=1, keepdims=True) * ROOT
        live = positions < prefix[n]
        top = jnp.maximum(
            jnp.max(jnp.where(live, scores, -jnp.inf), axis=1, keepdims=True), fresh_score
        )
        raised = jnp.where(live, jnp.exp(scores - top), 0.0)
        fresh_raised = jnp.exp(fresh_score - top)
        total = jnp.sum(raised, axis=1, keepdims=True) + fresh_raised
        weights = (raised / total).astype(bf16)
        fresh_weight = (fresh_raised / total).astype(bf16).astype(f32)
        mixed = dot(weights, vc[n, 1]) + fresh_weight * newest[2:3]
        attended[pl.ds(n, 1), :] = head_pick(mixed)
    loads[1].wait()
    pl.semaphore_wait(barrier, len(peers))
    own_sum = Spread(
        attended[...].astype(bf16), vs, part, red, full, [rsems.at[i] for i in range(4)]
    )
    own_sum.start()
    for i in range(8):
        wload[i].wait()
        flat = wbuf[i % 4].reshape(wstep, 512)
        at = pl.ds(i * wstep, wstep)
        wx[a, at, :] = flat
        if i + 4 < 8:
            wload[i + 4].start()
    ring = Ring(wx, a, by_a, rings, ringr)
    ring.start()
    loads[2].start()
    late = pltpu.make_async_copy(w_cross, vs, lsem.at[3])
    late.start()
    for i in range(10):
        tload[i].wait()
        wide[pl.ds(i * tstep, tstep), :] = tbuf[i % 5].astype(f32)
        if i + 5 < 10:
            tload[i + 5].start()

    def look(p):
        def some(k, c):
            for u in range(32):
                found[k * 32 + u, :] = wide[wanted[p, k, u], :]
            return c

        lax.fori_loop(0, CAP // 32, some, 0)
        return found[...].astype(bf16)

    sends = []

    def look_and_send(d):
        p = groups[d]
        rows[p] = look(p)
        copy = remote(rows.at[p], got.at[g], ysend.at[d], yrecv.at[d], {"grp": p})
        copy.start()
        sends.append(copy)

    listed.wait()
    for d in range(7):
        look_and_send(d)
        if d == 2:
            own_sum.share()
    ring.service()
    got[g] = look(g)
    own_sum.arrive()
    squares = jnp.zeros((8, 512), f32)
    for c in range(LANES):
        at = pl.ds(c * 512, 512)
        summed = full[c]
        delta[:, at] = summed.astype(bf16)
        r = hidden[:, at].astype(f32) + summed
        squares = squares + r * r
    scale = lax.rsqrt(jnp.sum(squares, axis=1, keepdims=True) / (LANES * 512) + epsilon)
    loads[2].wait()
    asked = jnp.zeros((8, 2 * HD), f32)
    for c in range(LANES):
        at = pl.ds(c * 512, 512)
        r = hidden[:, at].astype(f32) + full[c]
        normed = (r * scale * gain[:, at]).astype(bf16)
        asked = asked + dot(normed, vq[at, :])
    qall[g] = asked.astype(bf16).astype(f32)
    asks = []
    for d, p in enumerate(groups):
        copy = remote(qall.at[g], qall.at[g], qgsend.at[d], qgrecv.at[d], {"grp": p})
        copy.start()
        asks.append(copy)


    for copy in sends:
        copy.wait_recv()
    for s in range(GROUPS):
        wide[pl.ds(s * CAP, CAP), :] = got[s].astype(f32)

    def put(h, first):
        def beam(b, c):
            def some(k, c):
                line = (first + b) * 4 + h * 2 + k // 4
                column = lax.rem(k, 4) * 32
                for u in range(32):
                    found[k * 32 + u, :] = wide[place[line, column + u], :]
                return c

            lax.fori_loop(0, 8, some, 0)
            placed[h, first + b] = found[0:256, :].astype(bf16)
            return c

        lax.fori_loop(0, 4, beam, 0)

    move = Move(placed, mb, core, a, b, by_a, by_b, sibling, msems)
    put(0, 4 - 4 * core)
    move.exchange_other(0)
    put(0, 4 * core)
    move.exchange_own(0)
    put(1, 4 - 4 * core)
    move.exchange_other(1)
    move.gather(0)
    put(1, 4 * core)
    move.exchange_own(1)
    move.relay(0)
    move.gather(1)
    move.relay(1)
    for copy in asks:
        copy.wait_recv()
    numbers = lax.broadcasted_iota(jnp.int32, (16, 64), 0) + (g - core) * 8
    chosen = (numbers == beams[...]).astype(bf16)
    routed = dot(chosen, qall[...].reshape(64, 2 * HD).astype(bf16))
    qsent[...] = routed
    qa[a] = routed
    for d in range(1, 4):
        copy = remote(
            qsent, qa.at[a], qtsend.at[d - 1], qtrecv.at[d - 1], by_a(lax.rem(a + d, 4))
        )
        copy.start()
        asks.append(copy)
    ring.finish()

    def encode(h, side):
        def piece(p):
            i, j = p // 4 * (1 - core) + p % 4 * core, p % 4 * (1 - core) + p // 4 * core
            return mb[i, h, j, side]

        squares = jnp.zeros((256, HD), f32)
        for p in range(LANES):
            value = piece(p).astype(f32)
            squares = squares + value * value
        scale = lax.rsqrt(jnp.sum(squares, axis=1, keepdims=True) / DE + epsilon)
        for p in range(LANES):
            at = pl.ds(p * HD, HD)
            enc[:, at] = (piece(p).astype(f32) * scale * egain[:, at]).astype(bf16)

        def project(k, carry):
            pairs[side, h, k] = dot(enc[...], wx[k]).astype(bf16)
            return carry

        lax.fori_loop(0, 4, project, 0)

    tokens = lax.broadcasted_iota(jnp.int32, (8, KMAX * NLEN), 1)

    def attend(side):
        beam = side * 8 + core * 4 + a
        live = tokens < counts[(g - core) * 8 + beam] * NLEN
        for k in range(4):
            spread = head_rows(qa[k, pl.ds(beam, 1), :]).astype(bf16)
            scores = jnp.concatenate(
                [dot_t(spread, pairs[side, h, k, :, : 2 * HD]) for h in range(2)], axis=1
            )
            scores = jnp.where(live, scores * ROOT, -jnp.inf)
            raised = jnp.exp(scores - jnp.max(scores, axis=1, keepdims=True))
            weights = (raised / jnp.sum(raised, axis=1, keepdims=True)).astype(bf16)
            mixed = dot(weights[:, :256], pairs[side, 0, k, :, 2 * HD :])
            mixed = mixed + dot(weights[:, 256:], pairs[side, 1, k, :, 2 * HD :])
            answer = head_pick(mixed).astype(bf16).astype(f32)
            answers[k, pl.ds(side, 1), :] = answer

    move.arrive(0)
    encode(0, 0)
    encode(0, 1)
    for copy in asks[7:]:
        copy.wait_recv()
    move.arrive(1)
    encode(1, 0)
    attend(0)
    encode(1, 1)
    attend(1)
    replies = []
    for d in range(1, 4):
        p = lax.rem(a + d, 4)
        copy = remote(answers.at[p], ab.at[a], atsend.at[d - 1], atrecv.at[d - 1], by_a(p))
        copy.start()
        replies.append(copy)
    ab[a] = answers[a]
    for copy in replies:
        copy.wait_recv()
    aall[g] = jnp.concatenate([ab[k, 0:2] for k in range(4)], axis=0)
    returns = []
    for d, p in enumerate(groups):
        copy = remote(aall.at[g], aall.at[g], agsend.at[d], agrecv.at[d], {"grp": p})
        copy.start()
        returns.append(copy)
    late.wait()
    for copy in returns:
        copy.wait_recv()
    line = lax.broadcasted_iota(jnp.int32, (8, 64), 0)
    decoded = jnp.zeros((8, 64), jnp.int32)
    for j in range(8):
        beam = slots[g * 8 + j]
        held_at = (beam // 16 * 2 + beam // 4 % 2) * 8 + beam % 4 * 2 + beam // 8 % 2
        decoded = jnp.where(line == j, held_at, decoded)
    picks = (lax.broadcasted_iota(jnp.int32, (8, 64), 1) == decoded).astype(bf16)
    held = dot(picks, aall[...].reshape(64, 2 * HD).astype(bf16)).astype(bf16)
    cross_sum = Spread(held, vs, cpart, cred, cfull, [csems.at[i] for i in range(4)])
    cross_sum.start()
    cross_sum.share()
    cross_sum.arrive()
    for c in range(LANES):
        both = cfull[c].astype(f32)
        out[:, pl.ds(c * 512, 256)] = both[:8].astype(bf16)
        out[:, pl.ds(c * 512 + 256, 256)] = both[8:].astype(bf16)
    own_sum.finish()
    cross_sum.finish()
    move.finish()
    for copy in sends + asks + replies + returns:
        copy.wait_send()


def step(wanted, place, prefix, counts, slots, fresh, beams, hidden, gain, egain, *large):
    table, cached, w_self, w_query, w, w_cross = large
    chunk = pltpu.VMEM((LANES, 8, 512), f32)
    shape = jax.ShapeDtypeStruct(hidden.shape, bf16)
    return pl.pallas_call(
        step_kernel,
        out_shape=(shape, shape),
        in_specs=[ANY] + [SMEM] * 4 + [VMEM] * 5 + [ANY] * 6,
        out_specs=(VMEM, VMEM),
        scratch_shapes=[
            pltpu.SMEM((GROUPS, 32, 32), jnp.int32),
            pltpu.VMEM((5, table.shape[0] // 10, HD), bf16),
            pltpu.VMEM(table.shape, f32),
            pltpu.VMEM((CAP, HD), f32),
            pltpu.VMEM((GROUPS, CAP, HD), bf16),
            pltpu.VMEM((GROUPS, CAP, HD), bf16),
            pltpu.VMEM((4, DE // 8, 2, 2 * HD), bf16),
            pltpu.VMEM((4, DE, 4 * HD), bf16),
            pltpu.VMEM(cached.shape, bf16),
            pltpu.VMEM(w_self.shape, bf16),
            pltpu.VMEM(w_query.shape, bf16),
            pltpu.VMEM((8, 2 * HD), f32),
        ]
        + [chunk] * 5
        + [
            pltpu.VMEM((LANES, 16, 256), bf16),
            pltpu.VMEM((2, 8, 256, HD), bf16),
            pltpu.VMEM((4, 2, 4, 2, 256, HD), bf16),
            pltpu.VMEM((256, DE), bf16),
            pltpu.VMEM((2, 2, 4, 256, 4 * HD), bf16),
            pltpu.VMEM((GROUPS, 8, 2 * HD), f32),
            pltpu.VMEM((16, 2 * HD), f32),
            pltpu.VMEM((4, 16, 2 * HD), f32),
            pltpu.VMEM((4, 8, 2 * HD), f32),
            pltpu.VMEM((4, 8, 2 * HD), f32),
            pltpu.VMEM((GROUPS, 8, 2 * HD), f32),
            DMA((5,)),
            DMA((4,)),
            DMA((5,)),
            DMA((7,)),
            DMA((7,)),
            DMA((4, 15)),
            DMA((4, 15)),
            DMA((6,)),
            DMA((6,)),
            [DMA((2, 8)), DMA((2, 8)), DMA((2, 3)), DMA((2, 3)), DMA((2,))],
            DMA((7,)),
            DMA((7,)),
            DMA((3,)),
            DMA((3,)),
            DMA((3,)),
            DMA((3,)),
            DMA((7,)),
            DMA((7,)),
        ],
        compiler_params=params(0),
        name="step",
    )(wanted, place, prefix, counts, slots, fresh, beams, hidden, gain, egain, *large)


def hand_kernel(delta, out, delta_out, out_out):
    delta_out[...] = delta[...]
    out_out[...] = out[...]


def hand_over(delta, out):
    return pl.pallas_call(
        hand_kernel,
        out_shape=(jax.ShapeDtypeStruct(delta.shape, bf16),) * 2,
        in_specs=[VMEM, VMEM],
        out_specs=(VMEM, VMEM),
        name="hand_over",
    )(delta, out)


def local(
    neighbour_ids,
    neighbour_shard,
    neighbour_count,
    slot_beam,
    prefix_length,
    embed_table,
    encoder_gain,
    hidden_in,
    decoder_gain,
    fresh_projections,
    cached_pairs,
    w_self_out,
    w_query,
    w_pairs,
    w_cross_out,
):
    shards = neighbour_shard.reshape(neighbour_ids.shape)
    wanted, place = prepare(neighbour_ids, shards, neighbour_count[None, :])
    delta, out = step(
        wanted, place, prefix_length, neighbour_count, slot_beam, fresh_projections,
        slot_beam[None, :],        hidden_in, decoder_gain[None, :], encoder_gain[None, :],
        embed_table, cached_pairs, w_self_out, w_query, w_pairs, w_cross_out,
    )
    return hand_over(delta, out)


def solution(mesh):
    placed = (
        P(),
        P(),
        P(),
        P(),
        P("grp"),
        P("grp", "tp"),
        P(),
        P("grp", None),
        P(),
        P("grp", None, "tp"),
        P("grp", None, None, "tp"),
        P("tp", None),
        P(None, "tp"),
        P(None, None, "tp"),
        P("tp", None),
    )
    return jax.shard_map(
        local,
        mesh=mesh,
        in_specs=placed,
        out_specs=(P("grp", None), P("grp", None)),
        check_vma=False,
    )
```
